128 devices in a mesh: gx: 16 (over z_hi, y, core), gy: 8 (over x, z_lo).
Axes of the slice: x: 4, y: 4, z: 4 (z_hi: 2, z_lo: 2; z = z_hi * 2 + z_lo), core: 2. Of those that a mesh axis runs over, the one named last changes fastest.
Arguments:
- electric_forward: float32 [3, 256, 256, 128], P(None, 'gx', 'gy'), may hold values from -6 to 6
- magnetic_forward: float32 [3, 256, 256, 128], P(None, 'gx', 'gy'), may hold values from -6 to 6
- electric_adjoint: float32 [3, 256, 256, 128], P(None, 'gx', 'gy'), may hold values from -6 to 6
- magnetic_adjoint: float32 [3, 256, 256, 128], P(None, 'gx', 'gy'), may hold values from -6 to 6
- permittivity: float32 [256, 256, 128], P('gx', 'gy'), may hold values from 1 to 4
- pattern: float32 [16384, 256], P(('gx', 'gy')), may hold values from -6 to 6
- owners: int32 [16384, 1], P(('gx', 'gy')), may hold values from 0 to 127; in each aligned block of 128 rows (0 to 127, 128 to 255, ...) at most 2 rows name the same one
- tile_count: int32 [16384], P(('gx', 'gy')), may hold values from 1 to 256, as said below
- tile_start: int32 [16384], P(('gx', 'gy')), may hold values from 0 to 16128, as said below
Outputs:
- electric_final: float32 [3, 256, 256, 128], P(None, 'gx', 'gy')
- pattern_grad: float32 [16384, 256], P(('gx', 'gy'))
The draws below stay inside these ranges and needn't reach their ends.
Inputs may be any that keep to these rules, and one draw needn't show every extreme that they name: `owners`: among the 128 tiles of one device no owner is named more than 2 times. `tile_count`: some tile has 256 live cells and some has one. `tile_start`: every tile's cells stay inside its owner's design slab.
All inputs are finite; a program needn't handle non-finite values.
Results may differ from the reference program's by a relative error of at most 0.00014.
Values sent between devices are 32-bit elements; how exact they have to be, the bound alone decides.
No kernel may reach another device: no remote copies, remote signals or barrier semaphores. Data moves between devices by JAX's collectives and lax.ppermute only.
A program may use at most 64 MiB of HBM per device.

```python
import math
import jax
import jax.numpy as jnp
import numpy as np
from jax import lax

CX = 16
CY = 32
CZ = 128
DLAYERS = 32
STEPS = 2
TILE_CELLS = 256
TILES_DEV = 128
CAP = 2
TILES = 16384
NX = 256
NY = 256
N_GY = 8
DEVICES = 128


def draw_tile_count(key, part):
    key = jax.random.fold_in(key, 11)
    counts = jax.random.randint(key, (TILES,), 1, TILE_CELLS + 1, dtype=jnp.int32)
    return counts.at[0].set(TILE_CELLS).at[1].set(1)


def draw_tile_start(key, part):
    key = jax.random.fold_in(key, 23)
    highest = CX * CY * DLAYERS - TILE_CELLS
    starts = jax.random.randint(key, (TILES,), 0, highest + 1, dtype=jnp.int32)
    return starts.at[0].set(highest).at[1].set(0)


def shard_levels(stream_key, extent, cuts, least, largest):
    level = 1.0
    for dim, parts in cuts:
        steps = jax.random.uniform(jax.random.fold_in(jax.random.fold_in(stream_key, 6), dim), (parts,), jnp.float32, least / len(cuts), largest / len(cuts))
        level = level * jnp.repeat(jnp.exp(steps), extent[dim] // parts).reshape((-1,) + (1,) * (len(extent) - 1 - dim))
    return level


def shared_out(key, own, number, rows, count, top, most, skew):
    order = jax.random.permutation(key, count)
    heavy_load, ordinary = shares(count, rows * top, most, skew, True), shares(count, rows * top, most, skew, False)
    places = jnp.arange(count)

    def named(sizes, rotation):
        used = int((sizes > 0).sum())
        fixed = max(1, used // 4)
        passed = fixed + (places - fixed + rotation * (used - fixed)) % max(1, count - fixed)
        return jnp.zeros((count,), jnp.int32).at[order[jnp.where(places < fixed, places, passed)]].set(jnp.asarray(sizes, jnp.int32))

    sizes = jnp.where(number % 4 == 0, named(heavy_load, number // 4), named(ordinary, number - number // 4 - 1))
    mixed = jax.random.permutation(jax.random.fold_in(own, 3), count)
    giver, receiver = mixed[0:count // 2 * 2:2], mixed[1:count // 2 * 2:2]
    room = jnp.minimum(sizes[giver] - 1, most - sizes[receiver]) // 2
    room = jnp.where((giver == order[0]) | (receiver == order[0]) | (sizes[receiver] == 0), 0, jnp.maximum(room, 0))
    passed = jax.random.randint(jax.random.fold_in(own, 4), (count // 2,), 0, 1 << 20) % (room + 1)
    sizes = sizes.at[giver].add(-passed).at[receiver].add(passed)
    items = jnp.searchsorted(jnp.cumsum(sizes), jnp.arange(rows * top), side="right").astype(jnp.int32)
    grid = items.reshape(top, rows).T
    grid = grid[jax.random.permutation(jax.random.fold_in(own, 1), rows)]
    rotation = jax.random.randint(jax.random.fold_in(own, 2), (rows, 1), 0, top)
    return jnp.take_along_axis(grid, (jnp.arange(top)[None, :] + rotation) % top, axis=1)


def shares(amount, total, most, skew, full):
    loads = [(1 << 20) // math.isqrt(standing ** skew) + 1 for standing in range(1, amount + 1)]
    largest = most if full else min(most, max(-(-total // amount), total * loads[0] // sum(loads)))
    least = 1 if total - largest >= amount - 1 else 0
    given, surplus = [largest] + [least] * (amount - 1), total - largest - least * (amount - 1)
    while surplus > 0:
        movable = [i for i in range(1, amount) if given[i] < largest] or [i for i in range(1, amount) if given[i] < most]
        pool, left = sum([loads[i] for i in movable]), surplus
        for i in movable:
            addition = min(most - given[i], max(1, left * loads[i] // pool), surplus)
            given[i] = given[i] + addition
            surplus = surplus - addition
    return np.array(given)


def gaussian(stream_key, shape, width, limit, cuts=(), kind=jnp.bfloat16):
    entries = jax.random.normal(stream_key, shape, jnp.float32) * width
    if len(cuts) > 0:
        entries = shard_levels(stream_key, shape, cuts, -0.22, 0.18) * entries
    return jnp.clip(entries, min=-limit, max=limit).astype(kind)


def setup_inputs(seed: int = 0) -> dict:
    arg_keys = jax.random.split(jax.random.key(seed), 10)
    electric_forward = gaussian(arg_keys[0], (3, NX, NY, CZ), 1.0, 6.0, ((1, 16), (2, 8)), jnp.float32)
    magnetic_forward = gaussian(arg_keys[1], (3, NX, NY, CZ), 1.0, 6.0, ((1, 16), (2, 8)), jnp.float32)
    electric_adjoint = gaussian(arg_keys[2], (3, NX, NY, CZ), 1.0, 6.0, ((1, 16), (2, 8)), jnp.float32)
    magnetic_adjoint = gaussian(arg_keys[3], (3, NX, NY, CZ), 1.0, 6.0, ((1, 16), (2, 8)), jnp.float32)
    permittivity = jnp.clip(jnp.exp(math.log(4.0) - 1.3862944 * jax.random.uniform(arg_keys[4], (NX, NY, CZ), jnp.float32) ** shard_levels(arg_keys[4], (NX, NY, CZ), ((0, 16), (1, 8)), -0.2, 0.2)), 1.0, 4.0)
    pattern = gaussian(arg_keys[5], (TILES, TILE_CELLS), 1.0, 6.0, ((0, 128),), jnp.float32)
    owners_keys = jax.random.split(jax.random.fold_in(arg_keys[6], 1), TILES // TILES_DEV)
    owners_turns = jax.random.permutation(jax.random.fold_in(arg_keys[6], 3), TILES // TILES_DEV)
    owners = jax.vmap(lambda own, number: shared_out(jax.random.fold_in(arg_keys[6], 2), own, number, TILES_DEV, DEVICES, 1, CAP, 2))(owners_keys, owners_turns).reshape((TILES, 1))
    tile_count = draw_tile_count(jax.random.fold_in(arg_keys[9], 71), 0)
    tile_start = draw_tile_start(jax.random.fold_in(arg_keys[9], 71), 0)
    return dict(electric_forward=electric_forward, magnetic_forward=magnetic_forward, electric_adjoint=electric_adjoint, magnetic_adjoint=magnetic_adjoint, permittivity=permittivity, pattern=pattern, owners=owners, tile_count=tile_count, tile_start=tile_start)


courant = 0.5
angular = 0.9
contrast = 8.0


def forward_diff(values, axis):
    edge = jnp.zeros_like(lax.slice_in_dim(values, 0, 1, axis=axis))
    ahead = jnp.concatenate([lax.slice_in_dim(values, 1, values.shape[axis], axis=axis), edge], axis=axis)
    return ahead - values


def backward_diff(values, axis):
    edge = jnp.zeros_like(lax.slice_in_dim(values, 0, 1, axis=axis))
    behind = jnp.concatenate([edge, lax.slice_in_dim(values, 0, values.shape[axis] - 1, axis=axis)], axis=axis)
    return values - behind


def curl_electric(field):
    first = forward_diff(field[2], 1) - forward_diff(field[1], 2)
    second = forward_diff(field[0], 2) - forward_diff(field[2], 0)
    third = forward_diff(field[1], 0) - forward_diff(field[0], 1)
    return jnp.stack([first, second, third], axis=0)


def curl_magnetic(field):
    first = backward_diff(field[2], 1) - backward_diff(field[1], 2)
    second = backward_diff(field[0], 2) - backward_diff(field[2], 0)
    third = backward_diff(field[1], 0) - backward_diff(field[0], 1)
    return jnp.stack([first, second, third], axis=0)


def evolve(electric, magnetic, inverse, lower):
    cosine = jnp.zeros(electric.shape[:3] + (DLAYERS,), jnp.float32)
    sine = jnp.zeros(electric.shape[:3] + (DLAYERS,), jnp.float32)
    for moment in range(1, STEPS + 1):
        magnetic = magnetic - courant * curl_electric(electric)
        electric = electric + courant * inverse * curl_magnetic(magnetic)
        window = electric[:, :, :, lower:lower + DLAYERS]
        cosine = cosine + math.cos(angular * moment) * window
        sine = sine + math.sin(angular * moment) * window
    return electric, cosine, sine


def reference(electric_forward, magnetic_forward, electric_adjoint, magnetic_adjoint, permittivity, pattern, owners, tile_count, tile_start):
    offsets = jnp.arange(TILE_CELLS, dtype=jnp.int32)
    owner_id = owners[:, 0].astype(jnp.int32)
    block_x = owner_id // N_GY
    block_y = owner_id % N_GY
    position = tile_start[:, None] + offsets[None, :]
    local_x = position // (CY * DLAYERS)
    local_y = (position // DLAYERS) % CY
    layer = position % DLAYERS
    flat_index = ((block_x[:, None] * CX + local_x) * NY + block_y[:, None] * CY + local_y) * DLAYERS + layer
    flat_index = flat_index.astype(jnp.int32)
    within = offsets[None, :] < tile_count[:, None]
    placed = jnp.where(within, pattern, jnp.float32(0.0))
    density = jax.ops.segment_sum(placed.reshape(-1), flat_index.reshape(-1), num_segments=NX * NY * DLAYERS)
    sigma = jax.nn.sigmoid(density.reshape(NX, NY, DLAYERS))
    lower = (CZ - DLAYERS) // 2
    eps_total = permittivity.at[:, :, lower:lower + DLAYERS].add(contrast * sigma)
    inverse = 1.0 / eps_total
    electric_final, cos_fwd, sin_fwd = evolve(electric_forward, magnetic_forward, inverse, lower)
    unused, cos_adj, sin_adj = evolve(electric_adjoint, magnetic_adjoint, inverse, lower)
    gradient = contrast * sigma * (1.0 - sigma) * jnp.sum(cos_fwd * cos_adj + sin_fwd * sin_adj, axis=0)
    picked = gradient.reshape(-1)[flat_index]
    pattern_grad = jnp.where(within, picked, jnp.float32(0.0))
    return electric_final, pattern_grad
```

```python
import functools
import math

import jax
import jax.numpy as jnp
from jax import lax
from jax.experimental import pallas as pl
from jax.experimental.pallas import tpu as pltpu
from jax.sharding import PartitionSpec as P

F32 = jnp.float32
LANES = 128
LAYERS = 32
LOWER = 48
COURANT = 0.5
ANGULAR = 0.9
CONTRAST = 8.0
EXACT = lax.Precision.HIGHEST

NX, NY = 16, 32
EX, EY = 20, 40
UP_ROWS = 23
DOWN_ROWS = 17
ROWS = 16


def iota(shape, dim):
    return lax.broadcasted_iota(jnp.int32, shape, dim)


def params(limit):
    return pltpu.CompilerParams(vmem_limit_bytes=limit * 2**20)


def cost(micros):
    return pl.CostEstimate(flops=micros * 10**9, bytes_accessed=0, transcendentals=0)


def vmem():
    return pl.BlockSpec(memory_space=pltpu.VMEM)


def hbm():
    return pl.BlockSpec(memory_space=pltpu.HBM)


def shape(*dims):
    return jax.ShapeDtypeStruct(dims, F32)


def plan(to_next):
    if to_next:
        return [(0, 0, -2, 2), (0, 1, -2, 2), (0, 2, -2, 2), (1, 0, -1, 1), (1, 1, -2, 2), (1, 2, -2, 2)]
    return [(0, 0, 0, 1), (0, 1, 0, 2), (0, 2, 0, 2), (1, 0, 0, 1), (1, 1, 0, 1), (1, 2, 0, 1)]


def plan_y(to_next):
    if to_next:
        return [(0, 0, -2, 2), (0, 1, -2, 2), (0, 2, -2, 2), (1, 0, -2, 2), (1, 1, -1, 1), (1, 2, -2, 2)]
    return [(0, 0, 0, 2), (0, 1, 0, 1), (0, 2, 0, 2), (1, 0, 0, 1), (1, 1, 0, 1), (1, 2, 0, 1)]


def run_copies(pairs, sems):
    copies = [pltpu.make_async_copy(a, b, sems.at[i]) for i, (a, b) in enumerate(pairs)]
    for c in copies:
        c.start()
    for c in copies:
        c.wait()


def faces_x(ef, hf, ea, ha, perm, up, down, sems):
    pairs = []
    for to_next, out in ((True, up), (False, down)):
        at = 0
        for fields in ((ef, hf), (ea, ha)):
            for field, comp, first, count in plan(to_next):
                first = first % NX
                pairs.append((fields[field].at[comp, pl.ds(first, count)], out.at[pl.ds(at, count)]))
                at += count
        pairs.append((perm.at[pl.ds(NX - 1 if to_next else 0, 1)], out.at[pl.ds(at, 1)]))
    run_copies(pairs, sems)


def send_x(ef, hf, ea, ha, perm):
    return pl.pallas_call(
        faces_x,
        out_shape=(shape(UP_ROWS, NY, LANES), shape(DOWN_ROWS, NY, LANES)),
        in_specs=[hbm()] * 5,
        out_specs=(vmem(), vmem()),
        scratch_shapes=[pltpu.SemaphoreType.DMA((26,))],
        compiler_params=params(63),
        cost_estimate=cost(1),
        name="faces_x",
    )(ef, hf, ea, ha, perm)


def x_halo_pairs(dest, dest_perm, below, above, low, high):
    pairs = []
    rows = pl.ds(low, high - low)
    for from_prev, src in ((True, below), (False, above)):
        at = 0
        for evolution in range(2):
            for field, comp, first, count in plan(from_prev):
                place = first + 2 if from_prev else NX + 2 + first
                c = field * 6 + evolution * 3 + comp
                pairs.append(
                    (src.at[pl.ds(at, count), rows], dest.at[c, pl.ds(place, count), pl.ds(0, high - low)])
                )
                at += count
        place = 1 if from_prev else NX + 2
        pairs.append((src.at[pl.ds(at, 1), rows], dest_perm.at[pl.ds(place, 1), pl.ds(0, high - low)]))
    return pairs


def faces_y(ef, hf, ea, ha, perm, below, above, up, down, first, last, first_perm, last_perm, sems):
    pairs = []
    for dest, dest_perm, low in ((first, first_perm, 0), (last, last_perm, NY - 8)):
        rows = pl.ds(low, 8)
        for i, src in enumerate((ef, ea, hf, ha)):
            for comp in range(3):
                pairs.append((src.at[comp, :, rows], dest.at[i * 3 + comp, pl.ds(2, NX)]))
        pairs.append((perm.at[:, rows], dest_perm.at[pl.ds(2, NX)]))
        pairs += x_halo_pairs(dest, dest_perm, below, above, low, low + 8)
    run_copies(pairs, sems)
    for to_next, src, src_perm, out in (
        (True, last, last_perm, up),
        (False, first, first_perm, down),
    ):
        flat = src.reshape(12 * EX * 8, LANES)
        flat_perm = src_perm.reshape(EX * 8, LANES)
        at = 0
        for evolution in range(2):
            for field, comp, begin, count in plan_y(to_next):
                for k in range(count):
                    row = (begin + k) % 8
                    c = field * 6 + evolution * 3 + comp
                    out[pl.ds(at * EX, EX), :] = flat[pl.ds(c * EX * 8 + row, EX, stride=8), :]
                    at += 1
        out[pl.ds(at * EX, EX), :] = flat_perm[pl.ds(7 if to_next else 0, EX, stride=8), :]


def send_y(ef, hf, ea, ha, perm, below, above):
    return pl.pallas_call(
        faces_y,
        out_shape=(shape(UP_ROWS * EX, LANES), shape(DOWN_ROWS * EX, LANES)),
        in_specs=[hbm()] * 5 + [vmem()] * 2,
        out_specs=(vmem(), vmem()),
        scratch_shapes=[
            pltpu.VMEM((12, EX, 8, LANES), F32),
            pltpu.VMEM((12, EX, 8, LANES), F32),
            pltpu.VMEM((EX, 8, LANES), F32),
            pltpu.VMEM((EX, 8, LANES), F32),
            pltpu.SemaphoreType.DMA((78,)),
        ],
        compiler_params=params(63),
        cost_estimate=cost(200),
        name="faces_y",
    )(ef, hf, ea, ha, perm, below, above)


def pack_tiles(pattern, owner, count, start, message, match):
    tiles = pattern.shape[0]
    square = (tiles, tiles)
    down, across = iota(square, 0), iota(square, 1)
    eye = down == across

    def column(row):
        return jnp.sum(jnp.where(eye, row.astype(F32), 0.0), axis=1, keepdims=True)

    owner_row = owner[...].astype(F32)
    owner_col = column(owner[...])
    same = owner_col == owner_row
    rank_row = jnp.sum(jnp.where(same & (down < across), 1.0, 0.0), axis=0, keepdims=True)
    rank_col = jnp.sum(jnp.where(same & (across < down), 1.0, 0.0), axis=1, keepdims=True)
    down_f, across_f = down.astype(F32), across.astype(F32)
    for k in range(2):
        match[:, k * tiles : (k + 1) * tiles] = jnp.where(
            (owner_col == across_f) & (rank_col == k), 1.0, 0.0
        )
    starts = column(start[...]).astype(jnp.int32)
    counts = column(count[...]).astype(jnp.int32)
    shift = starts & (LANES - 1)
    first = starts >> 7
    phase = first & 7
    wide = iota(pattern.shape, 1)
    cells = jnp.where(wide < counts, pattern[...], 0.0)
    for bit in range(7):
        cells = jnp.where((shift >> bit) & 1 == 1, pltpu.roll(cells, 1 << bit, 1), cells)
    front, back = cells[:, :LANES], cells[:, LANES:]
    head = jnp.where(across >= shift, front, 0.0)
    tail = jnp.where(across >= shift, 0.0, front)

    def pick(a, b, c):
        return jnp.where(
            phase == a, head, jnp.where(phase == b, back, jnp.where(phase == c, tail, 0.0))
        )

    low_y = pick(0, 7, 6)
    high_y = pick(7, 6, 5)
    low_corner = pltpu.roll(jnp.where((first + 7) >> 3 == NX - 1, low_y, 0.0), 32, 1)
    high_corner = pltpu.roll(jnp.where(first >> 3 == 0, high_y, 0.0), 96, 1)
    edges = jnp.where(
        across < 32,
        low_y,
        jnp.where(across < 64, low_corner, jnp.where(across < 96, high_corner, high_y)),
    )
    origin = jnp.broadcast_to(starts.astype(F32), square)
    everything = jnp.concatenate([front, back, edges, origin], axis=1)
    meta = jnp.zeros(square, F32)
    for k in range(2):
        choose = jnp.where((owner_row == down_f) & (rank_row == k), 1.0, 0.0)
        slots = jnp.dot(choose, everything, precision=EXACT, preferred_element_type=F32)
        pair = slots[:, : 2 * LANES]
        edge = slots[:, 2 * LANES : 3 * LANES]
        origins = slots[:, 3 * LANES :]

        def other(values, distance):
            return pltpu.roll(values, -distance % tiles, 0)

        for place, distance in ((0, 0), (4, 8), (8, -8)):
            rows = other(pair, distance) if distance else pair
            for half in range(2):
                message[pl.ds(place + 2 * k + half, tiles, stride=ROWS), :] = rows[
                    :, half * LANES : (half + 1) * LANES
                ]
        message[pl.ds(12 + k, tiles, stride=ROWS), :] = jnp.where(
            across < 32,
            other(edge, 1),
            jnp.where(across < 64, other(edge, -7), jnp.where(across < 96, other(edge, 7), other(edge, -1))),
        )
        for place, distance in enumerate((0, 8, -8, 1, -1)):
            moved = other(origins, distance) if distance else origins
            meta = jnp.where(across == 2 * place + k, moved, meta)
    message[pl.ds(14, tiles, stride=ROWS), :] = meta
    message[pl.ds(15, tiles, stride=ROWS), :] = jnp.zeros(square, F32)


def pack(pattern, owners, tile_count, tile_start):
    tiles = pattern.shape[0]
    return pl.pallas_call(
        pack_tiles,
        out_shape=(shape(tiles * ROWS, LANES), shape(tiles, 2 * tiles)),
        in_specs=[vmem()] * 4,
        out_specs=(vmem(), vmem()),
        compiler_params=params(16),
        cost_estimate=cost(2),
        name="pack_tiles",
    )(pattern, owners.reshape(1, tiles), tile_count.reshape(1, tiles), tile_start.reshape(1, tiles))


def after_y(values):
    return pltpu.roll(values, values.shape[0] - 1, 0)


def before_y(values):
    return pltpu.roll(values, 1, 0)


def after_z(values):
    return jnp.where(iota(values.shape, 1) == LANES - 1, 0.0, pltpu.roll(values, LANES - 1, 1))


def before_z(values):
    return jnp.where(iota(values.shape, 1) == 0, 0.0, pltpu.roll(values, 1, 1))


def curl_e(here, ahead):
    ex, ey, ez = here
    next_y, next_z = ahead
    return (
        (after_y(ez) - ez) - (after_z(ey) - ey),
        (after_z(ex) - ex) - (next_z - ez),
        (next_y - ey) - (after_y(ex) - ex),
    )


def curl_h(here, behind):
    hx, hy, hz = here
    last_y, last_z = behind
    return (
        (hz - before_y(hz)) - (hy - before_z(hy)),
        (hx - before_z(hx)) - (hz - last_z),
        (hy - last_y) - (hx - before_y(hx)),
    )


def evolve(
    ef, hf, ea, ha, perm, below, above, before, after, message,
    final, reply,
    fields, perm_wide, rate, grow, turned, overlap, sems,
):
    pairs = []
    for i, src in enumerate((ef, ea, hf, ha)):
        for comp in range(3):
            pairs.append((src.at[comp], fields.at[i * 3 + comp, pl.ds(2, NX), pl.ds(0, NY)]))
    pairs.append((perm, perm_wide.at[pl.ds(2, NX), pl.ds(0, NY)]))
    pairs += x_halo_pairs(fields, perm_wide, below, above, 0, NY)
    copies = [pltpu.make_async_copy(a, b, sems.at[i]) for i, (a, b) in enumerate(pairs)]
    for copy in copies:
        copy.start()
    tiles = message.shape[0] // ROWS
    square = (tiles, LANES)
    across = iota(square, 1)

    def rows_of(place):
        return message[pl.ds(place, tiles, stride=ROWS), :]

    meta = rows_of(14)
    meta_rows = meta.T

    def start_row(index):
        return meta_rows[index : index + 1, :].astype(jnp.int32)

    def start_col(index):
        return meta[:, index : index + 1].astype(jnp.int32)

    def place_cells(place, index, base, count):
        targets, values = [], []
        for k in range(2):
            first = start_row(index + k) >> 7
            shift = start_col(index + k) & (LANES - 1)
            front, back = rows_of(place + 2 * k), rows_of(place + 2 * k + 1)
            for step, part in enumerate(
                (
                    jnp.where(across >= shift, front, 0.0),
                    back,
                    jnp.where(across >= shift, 0.0, front),
                )
            ):
                row = iota((count, tiles), 0) + base
                targets.append(jnp.where(first + step == row, 1.0, 0.0))
                values.append(part)
        return jnp.dot(
            jnp.concatenate(targets, axis=1),
            jnp.concatenate(values, axis=0),
            precision=EXACT,
            preferred_element_type=F32,
        )

    def lift(density):
        return CONTRAST * jax.nn.sigmoid(density)

    block = NX * 8
    sigma = jax.nn.sigmoid(place_cells(0, 0, 0, block))
    own = CONTRAST * sigma
    ahead = lift(place_cells(4, 2, 0, 8))
    behind = lift(place_cells(8, 4, block - 8, 8))
    targets = []
    for k in range(2):
        first = start_row(6 + k) >> 7
        last = start_row(8 + k) >> 7
        row = iota((40, tiles), 0)
        targets.append(
            jnp.where(
                (((first + 7) >> 3 == row) & (row < NX))
                | ((last >> 3) + NX == row)
                | (row >= 2 * NX),
                1.0,
                0.0,
            )
        )
    sides = lift(
        jnp.dot(
            jnp.concatenate(targets, axis=1),
            jnp.concatenate([rows_of(12), rows_of(13)], axis=0),
            precision=EXACT,
            preferred_element_type=F32,
        )
    )

    def lanes_to(values, source):
        lane = iota(values.shape, 1)
        moved = pltpu.roll(values, (LOWER - source) % LANES, 1)
        return jnp.where((lane >= LOWER) & (lane < LOWER + LAYERS), moved, 0.0)

    grow[...] = jnp.zeros_like(grow)
    for quarter in range(4):
        source = quarter * LAYERS
        moved = lanes_to(own, source)
        for x in range(NX):
            grow[pl.ds((x + 2) * EY + quarter, 8, stride=4), :] = moved[8 * x : 8 * x + 8]
        grow[pl.ds((NX + 2) * EY + quarter, 8, stride=4), :] = lanes_to(ahead, source)
        grow[pl.ds(EY + quarter, 8, stride=4), :] = lanes_to(behind, source)
    grow[pl.ds(2 * EY + NY, NX, stride=EY), :] = lanes_to(sides[:NX], 0)
    grow[pl.ds(2 * EY + EY - 1, NX, stride=EY), :] = lanes_to(sides[NX : 2 * NX], 96)
    corner = sides[2 * NX : 2 * NX + 8]
    grow[pl.ds(EY + NY, 1), :] = lanes_to(corner, 32)[:1]
    grow[pl.ds((NX + 2) * EY + EY - 1, 1), :] = lanes_to(corner, 64)[:1]

    gx, gy = lax.axis_index("gx"), lax.axis_index("gy")
    low_x, high_x = gx > 0, gx < lax.axis_size("gx") - 1
    low_y, high_y = gy > 0, gy < lax.axis_size("gy") - 1
    y = iota((EY, LANES), 0)
    within = (y < NY) | ((y == NY) & high_y) | ((y == EY - 1) & low_y)


    for copy in copies:
        copy.wait()
    flat = fields.reshape(12 * EX * EY, LANES)
    flat_perm = perm_wide.reshape(EX * EY, LANES)
    for from_prev, src in ((True, before), (False, after)):
        at = 0
        for evolution in range(2):
            for field, comp, begin, count in plan_y(from_prev):
                for k in range(count):
                    row = EY + begin + k if from_prev else NY + begin + k
                    c = field * 6 + evolution * 3 + comp
                    flat[pl.ds(c * EX * EY + row, EX, stride=EY), :] = src[pl.ds(at * EX, EX), :]
                    at += 1
        row = EY - 1 if from_prev else NY
        flat_perm[pl.ds(row, EX, stride=EY), :] = src[pl.ds(at * EX, EX), :]
    cut = jnp.where((y < EY - 2) | low_y, COURANT, 0.0)

    for x in range(NX + 3):
        factor = cut if x >= 2 else jnp.where(low_x, cut, 0.0)
        for e in (0, 3):
            here = [fields[e + c, x] for c in range(3)]
            curl = curl_e(here, [fields[e + c, x + 1] for c in (1, 2)])
            for c in range(3):
                turned[6 + e + c, x] = fields[6 + e + c, x] - factor * curl[c]
    for x in range(1, NX + 3):
        eps = perm_wide[x] + grow[pl.ds(x * EY, EY), :]
        inside = within
        if x == 1:
            inside = within & low_x
        if x == NX + 2:
            inside = within & high_x
        scale = jnp.where(inside, COURANT / eps, 0.0)
        rate[x] = scale
        for e in (0, 3):
            here = [turned[6 + e + c, x] for c in range(3)]
            curl = curl_h(here, [turned[6 + e + c, x - 1] for c in (1, 2)])
            for c in range(3):
                turned[e + c, x] = fields[e + c, x] + scale * curl[c]
    for x in range(1, NX + 2):
        factor = cut if x >= 2 else jnp.where(low_x, cut, 0.0)
        for e in (0, 3):
            here = [turned[e + c, x] for c in range(3)]
            curl = curl_e(here, [turned[e + c, x + 1] for c in (1, 2)])
            for c in range(3):
                fields[6 + e + c, x] = turned[6 + e + c, x] - factor * curl[c]
    blend = math.cos(ANGULAR)
    for x in range(2, NX + 2):
        scale = rate[x]
        old, new = [], []
        for e in (0, 3):
            here = [fields[6 + e + c, x] for c in range(3)]
            curl = curl_h(here, [fields[6 + e + c, x - 1] for c in (1, 2)])
            old.append([turned[e + c, x][:NY] for c in range(3)])
            new.append([old[-1][c] + (scale * curl[c])[:NY] for c in range(3)])
        total = 0.0
        for c in range(3):
            final[c, x - 2] = new[0][c]
            total += old[0][c] * (old[1][c] + blend * new[1][c])
            total += new[0][c] * (new[1][c] + blend * old[1][c])
        overlap[pl.ds((x - 2) * NY, NY), :] = total
    compact = jnp.zeros((block, LANES), F32)
    lane = iota((block, LANES), 1)
    for quarter in range(4):
        part = pltpu.roll(
            overlap[pl.ds(quarter, block, stride=4), :], (quarter * LAYERS - LOWER) % LANES, 1
        )
        compact = jnp.where(lane // LAYERS == quarter, part, compact)
    gradient = own * (1.0 - sigma) * compact
    for k in range(2):
        starts = start_col(k)
        first, shift = starts >> 7, starts & (LANES - 1)
        picks = [jnp.where(iota((tiles, block), 1) == first + step, 1.0, 0.0) for step in range(3)]
        found = jnp.dot(
            jnp.concatenate(picks, axis=0), gradient, precision=EXACT, preferred_element_type=F32
        )
        reply[pl.ds(2 * k, tiles, stride=4), :] = jnp.where(
            across >= shift, found[:tiles], found[2 * tiles :]
        )
        reply[pl.ds(2 * k + 1, tiles, stride=4), :] = found[tiles : 2 * tiles]


def run_fields(ef, hf, ea, ha, perm, below, above, before, after, message):
    tiles = message.shape[0] // ROWS
    return pl.pallas_call(
        evolve,
        out_shape=(shape(3, NX, NY, LANES), shape(tiles * 4, LANES)),
        in_specs=[hbm()] * 5 + [vmem()] * 5,
        out_specs=(vmem(), vmem()),
        scratch_shapes=[
            pltpu.VMEM((12, EX, EY, LANES), F32),
            pltpu.VMEM((EX, EY, LANES), F32),
            pltpu.VMEM((EX, EY, LANES), F32),
            pltpu.VMEM((EX * EY, LANES), F32),
            pltpu.VMEM((12, EX, EY, LANES), F32),
            pltpu.VMEM((NX * NY, LANES), F32),
            pltpu.SemaphoreType.DMA((39,)),
        ],
        compiler_params=params(63),
        cost_estimate=cost(8),
        name="evolve",
    )(ef, hf, ea, ha, perm, below, above, before, after, message)


def unpack_tiles(reply, match, count, start, out):
    tiles = out.shape[0]
    eye = iota((tiles, tiles), 0) == iota((tiles, tiles), 1)

    def column(row):
        values = jnp.sum(jnp.where(eye, row.astype(F32), 0.0), axis=1, keepdims=True)
        return values.astype(jnp.int32)

    shift = column(start[...]) & (LANES - 1)
    rows = [
        jnp.concatenate(
            [reply[pl.ds(2 * k + half, tiles, stride=4), :] for half in range(2)], axis=1
        )
        for k in range(2)
    ]
    cells = jnp.dot(
        match[...], jnp.concatenate(rows, axis=0), precision=EXACT, preferred_element_type=F32
    )
    width = out.shape[1]
    for bit in range(7):
        cells = jnp.where((shift >> bit) & 1 == 1, pltpu.roll(cells, width - (1 << bit), 1), cells)
    out[...] = jnp.where(iota(out.shape, 1) < column(count[...]), cells, 0.0)


def unpack(reply, match, tile_count, tile_start):
    tiles = match.shape[0]
    return pl.pallas_call(
        unpack_tiles,
        out_shape=shape(tiles, 2 * LANES),
        in_specs=[vmem()] * 4,
        out_specs=vmem(),
        compiler_params=params(16),
        cost_estimate=cost(2),
        name="unpack_tiles",
    )(reply, match, tile_count.reshape(1, tiles), tile_start.reshape(1, tiles))


def passed(block, axis, distance):
    devices = range(lax.axis_size(axis))
    return lax.ppermute(
        block, axis, [(i, i + distance) for i in devices if i + distance in devices]
    )


def exchange(block, rows):
    tiles = block.shape[0] // rows
    out = lax.all_to_all(
        block.reshape(tiles, rows, LANES), ("gx", "gy"), split_axis=0, concat_axis=0, tiled=True
    )
    return out.reshape(tiles * rows, LANES)


def shards(ef, hf, ea, ha, perm, pattern, owners, tile_count, tile_start):
    up, down = send_x(ef, hf, ea, ha, perm)
    up, down, pattern = lax.optimization_barrier((up, down, pattern))
    below, above = passed(up, "gx", 1), passed(down, "gx", -1)
    message, match = pack(pattern, owners, tile_count, tile_start)
    arrived = exchange(message, ROWS)
    up, down = send_y(ef, hf, ea, ha, perm, below, above)
    before, after = passed(up, "gy", 1), passed(down, "gy", -1)
    final, reply = run_fields(ef, hf, ea, ha, perm, below, above, before, after, arrived)
    returned = exchange(reply, 4)
    return final, unpack(returned, match, tile_count, tile_start)


def solution(mesh):
    grid = P(None, "gx", "gy", None)
    tiles = ("gx", "gy")
    return jax.shard_map(
        shards,
        mesh=mesh,
        in_specs=(grid,) * 4 + (P("gx", "gy", None), P(tiles, None), P(tiles, None), P(tiles), P(tiles)),
        out_specs=(grid, P(tiles, None)),
        check_vma=False,
    )
```

```python
import functools
import math

import jax
import jax.numpy as jnp
from jax import lax
from jax.experimental import pallas as pl
from jax.experimental.pallas import tpu as pltpu
from jax.sharding import PartitionSpec as P

F32 = jnp.float32
LANES = 128
LAYERS = 32
LOWER = 48
COURANT = 0.5
ANGULAR = 0.9
CONTRAST = 8.0
EXACT = lax.Precision.HIGHEST

NX, NY = 16, 32
EX, EY = 20, 40
UP_ROWS = 23
DOWN_ROWS = 17
ROWS = 15


def iota(shape, dim):
    return lax.broadcasted_iota(jnp.int32, shape, dim)


def params(limit):
    return pltpu.CompilerParams(vmem_limit_bytes=limit * 2**20)


def cost(micros):
    return pl.CostEstimate(flops=micros * 10**9, bytes_accessed=0, transcendentals=0)


def vmem():
    return pl.BlockSpec(memory_space=pltpu.VMEM)


def anywhere():
    return pl.BlockSpec(memory_space=pl.ANY)


def hbm():
    return pl.BlockSpec(memory_space=pltpu.HBM)


def shape(*dims):
    return jax.ShapeDtypeStruct(dims, F32)


def select_rows(marks, values):
    width = values.shape[1]
    high = values.astype(jnp.bfloat16)
    low = (values - high.astype(F32)).astype(jnp.bfloat16)
    found = jnp.dot(
        marks.astype(jnp.bfloat16),
        jnp.concatenate([high, low], axis=1),
        preferred_element_type=F32,
    )
    return found[:, :width] + found[:, width:]


def plan(to_next):
    if to_next:
        return [(0, 0, -2, 2), (0, 1, -2, 2), (0, 2, -2, 2), (1, 0, -1, 1), (1, 1, -2, 2), (1, 2, -2, 2)]
    return [(0, 0, 0, 1), (0, 1, 0, 2), (0, 2, 0, 2), (1, 0, 0, 1), (1, 1, 0, 1), (1, 2, 0, 1)]


def plan_y(to_next):
    if to_next:
        return [(0, 0, -2, 2), (0, 1, -2, 2), (0, 2, -2, 2), (1, 0, -2, 2), (1, 1, -1, 1), (1, 2, -2, 2)]
    return [(0, 0, 0, 2), (0, 1, 0, 1), (0, 2, 0, 2), (1, 0, 0, 1), (1, 1, 0, 1), (1, 2, 0, 1)]


def pack_tiles(pattern, owner, count, start, message, match):
    tiles = pattern.shape[0]
    square = (tiles, tiles)
    down, across = iota(square, 0), iota(square, 1)
    eye = down == across

    def column(row):
        return jnp.sum(jnp.where(eye, row.astype(F32), 0.0), axis=1, keepdims=True)

    owner_row = owner[...].astype(F32)
    owner_col = column(owner[...])
    same = owner_col == owner_row
    rank_row = jnp.sum(jnp.where(same & (down < across), 1.0, 0.0), axis=0, keepdims=True)
    rank_col = jnp.sum(jnp.where(same & (across < down), 1.0, 0.0), axis=1, keepdims=True)
    down_f, across_f = down.astype(F32), across.astype(F32)
    for k in range(2):
        match[:, k * tiles : (k + 1) * tiles] = jnp.where(
            (owner_col == across_f) & (rank_col == k), 1.0, 0.0
        )
    starts = column(start[...]).astype(jnp.int32)
    counts = column(count[...]).astype(jnp.int32)
    shift = starts & (LANES - 1)
    first = starts >> 7
    phase = first & 7
    match[:, 2 * tiles :] = jnp.where(
        across == 0, shift.astype(F32), jnp.where(across == 1, counts.astype(F32), 0.0)
    )
    wide = iota(pattern.shape, 1)
    cells = jnp.where(wide < counts, pattern[...], 0.0)
    for bit in range(7):
        cells = jnp.where((shift >> bit) & 1 == 1, pltpu.roll(cells, 1 << bit, 1), cells)
    front, back = cells[:, :LANES], cells[:, LANES:]
    head = jnp.where(across >= shift, front, 0.0)
    tail = jnp.where(across >= shift, 0.0, front)

    def pick(a, b, c):
        return jnp.where(
            phase == a, head, jnp.where(phase == b, back, jnp.where(phase == c, tail, 0.0))
        )

    low_y = pick(0, 7, 6)
    high_y = pick(7, 6, 5)
    low_corner = pltpu.roll(jnp.where((first + 7) >> 3 == NX - 1, low_y, 0.0), 32, 1)
    high_corner = pltpu.roll(jnp.where(first >> 3 == 0, high_y, 0.0), 96, 1)
    edges = jnp.where(
        across < 32,
        low_y,
        jnp.where(across < 64, low_corner, jnp.where(across < 96, high_corner, high_y)),
    )
    origin = jnp.broadcast_to(starts.astype(F32), square)
    everything = jnp.concatenate([front, back, edges, origin], axis=1)
    meta = jnp.zeros(square, F32)
    choose = [jnp.where((owner_row == down_f) & (rank_row == k), 1.0, 0.0) for k in range(2)]
    every_slot = select_rows(jnp.concatenate(choose, axis=0), everything)
    for k in range(2):
        slots = every_slot[k * tiles : (k + 1) * tiles]
        pair = slots[:, : 2 * LANES]
        edge = slots[:, 2 * LANES : 3 * LANES]
        origins = slots[:, 3 * LANES :]

        def other(values, distance):
            return pltpu.roll(values, -distance % tiles, 0)

        for place, distance in ((0, 0), (4, 8), (8, -8)):
            rows = other(pair, distance) if distance else pair
            for half in range(2):
                message[pl.ds(place + 2 * k + half, tiles, stride=ROWS), :] = rows[
                    :, half * LANES : (half + 1) * LANES
                ]
        message[pl.ds(12 + k, tiles, stride=ROWS), :] = jnp.where(
            across < 32,
            other(edge, 1),
            jnp.where(across < 64, other(edge, -7), jnp.where(across < 96, other(edge, 7), other(edge, -1))),
        )
        for place, distance in enumerate((0, 8, -8, 1, -1)):
            moved = other(origins, distance) if distance else origins
            meta = jnp.where(across == 2 * place + k, moved, meta)
    message[pl.ds(14, tiles, stride=ROWS), :] = meta


def prepare_all(
    ef, hf, ea, ha, perm, pattern_hbm, owner_hbm, count_hbm, start_hbm,
    up_x, down_x, up_y, down_y, message, match,
    first, last, first_perm, last_perm, first_x, last_x, first_x_perm, last_x_perm,
    pattern, owner, count, start, sems,
):
    small = [(owner_hbm, owner), (count_hbm, count), (start_hbm, start), (pattern_hbm, pattern)]
    loads_x, loads_y = [], []
    for begin, out, out_perm in ((NX - 2, last_x, last_x_perm), (0, first_x, first_x_perm)):
        for i, src in enumerate((ef, ea, hf, ha)):
            loads_x.append((src.at[:, pl.ds(begin, 2)], out.at[pl.ds(3 * i, 3)]))
        loads_x.append((perm.at[pl.ds(begin, 2)], out_perm))
    for dest, dest_perm, low in ((first, first_perm, 0), (last, last_perm, NY - 8)):
        rows = pl.ds(low, 8)
        for i, src in enumerate((ef, ea, hf, ha)):
            loads_y.append((src.at[:, :, rows], dest.at[pl.ds(3 * i, 3)]))
        loads_y.append((perm.at[:, rows], dest_perm))
    copies = [
        pltpu.make_async_copy(a, b, sems.at[i]) for i, (a, b) in enumerate(small + loads_y + loads_x)
    ]
    for copy in copies:
        copy.start()
    for copy in copies[:4]:
        copy.wait()
    pack_tiles(pattern, owner, count, start, message, match)
    for copy in copies[4:]:
        copy.wait()
    for to_next, src, src_perm, out in ((True, last, last_perm, up_y), (False, first, first_perm, down_y)):
        flat = src.reshape(12 * NX * 8, LANES)
        flat_perm = src_perm.reshape(NX * 8, LANES)
        at = 0
        for evolution in range(2):
            for field, comp, begin, planes in plan_y(to_next):
                for k in range(planes):
                    row = (field * 6 + evolution * 3 + comp) * NX * 8 + (begin + k) % 8
                    out[pl.ds(at * NX, NX), :] = flat[pl.ds(row, NX, stride=8), :]
                    at += 1
        out[pl.ds(at * NX, NX), :] = flat_perm[pl.ds(7 if to_next else 0, NX, stride=8), :]
    for to_next, src, src_perm, out in (
        (True, last_x, last_x_perm, up_x),
        (False, first_x, first_x_perm, down_x),
    ):
        at = 0
        for evolution in range(2):
            for field, comp, begin, planes in plan(to_next):
                for k in range(planes):
                    out[at] = src[field * 6 + evolution * 3 + comp, (begin + k) % 2]
                    at += 1
        out[at] = src_perm[1 if to_next else 0]


def prepare(ef, hf, ea, ha, perm, pattern, owners, tile_count, tile_start):
    tiles = pattern.shape[0]
    return pl.pallas_call(
        prepare_all,
        out_shape=(
            shape(UP_ROWS, NY, LANES),
            shape(DOWN_ROWS, NY, LANES),
            shape(UP_ROWS * NX, LANES),
            shape(DOWN_ROWS * NX, LANES),
            shape(tiles * ROWS, LANES),
            shape(tiles, 3 * tiles),
        ),
        in_specs=[hbm()] * 9,
        out_specs=(vmem(),) * 6,
        scratch_shapes=[
            pltpu.VMEM((12, NX, 8, LANES), F32),
            pltpu.VMEM((12, NX, 8, LANES), F32),
            pltpu.VMEM((NX, 8, LANES), F32),
            pltpu.VMEM((NX, 8, LANES), F32),
            pltpu.VMEM((12, 2, NY, LANES), F32),
            pltpu.VMEM((12, 2, NY, LANES), F32),
            pltpu.VMEM((2, NY, LANES), F32),
            pltpu.VMEM((2, NY, LANES), F32),
            pltpu.VMEM((tiles, 2 * LANES), F32),
            pltpu.VMEM((1, tiles), jnp.int32),
            pltpu.VMEM((1, tiles), jnp.int32),
            pltpu.VMEM((1, tiles), jnp.int32),
            pltpu.SemaphoreType.DMA((24,)),
        ],
        compiler_params=params(56),
        cost_estimate=cost(3),
        name="prepare",
    )(
        ef, hf, ea, ha, perm, pattern,
        owners.reshape(1, tiles), tile_count.reshape(1, tiles), tile_start.reshape(1, tiles),
    )


def after_y(values):
    return pltpu.roll(values, values.shape[0] - 1, 0)


def before_y(values):
    return pltpu.roll(values, 1, 0)


def after_z(values):
    return jnp.where(iota(values.shape, 1) == LANES - 1, 0.0, pltpu.roll(values, LANES - 1, 1))


def before_z(values):
    return jnp.where(iota(values.shape, 1) == 0, 0.0, pltpu.roll(values, 1, 1))


def curl_e(here, ahead):
    ex, ey, ez = here
    next_y, next_z = ahead
    return (
        (after_y(ez) - ez) - (after_z(ey) - ey),
        (after_z(ex) - ex) - (next_z - ez),
        (next_y - ey) - (after_y(ex) - ex),
    )


def curl_h(here, behind):
    hx, hy, hz = here
    last_y, last_z = behind
    return (
        (hz - before_y(hz)) - (hy - before_z(hy)),
        (hx - before_z(hx)) - (hz - last_z),
        (hy - last_y) - (hx - before_y(hx)),
    )


def evolve(
    ef, hf, ea, ha, perm, below_any, above_any, before_any, after_any, low_any, high_any, message_any,
    final, reply,
    final_v, forward, adjoint, perm_wide, rate, grow, turned, overlap, below, above, before, after, low, high, message, sems,
):
    wide = (forward, adjoint)
    pairs = [
        (message_any, message),
        (below_any, below),
        (above_any, above),
        (before_any, before),
        (after_any, after),
        (low_any, low),
        (high_any, high),
    ]
    pairs.append((perm, perm_wide.at[pl.ds(2, NX), pl.ds(0, NY)]))
    for i, src in ((0, ef), (1, hf), (2, ea), (3, ha)):
        pairs.append((src, wide[i // 2].at[pl.ds(3 * (i % 2), 3), pl.ds(2, NX), pl.ds(0, NY)]))
    copies = [pltpu.make_async_copy(a, b, sems.at[i]) for i, (a, b) in enumerate(pairs)]
    for copy in copies:
        copy.start()
    final_copy = pltpu.make_async_copy(final_v, final, sems.at[12])
    copies[0].wait()
    tiles = message.shape[0] // ROWS
    square = (tiles, LANES)
    across = iota(square, 1)

    def rows_of(place):
        return message[pl.ds(place, tiles, stride=ROWS), :]

    meta = rows_of(14)
    meta_rows = meta.T

    def start_row(index):
        return meta_rows[index : index + 1, :].astype(jnp.int32)

    def start_col(index):
        return meta[:, index : index + 1].astype(jnp.int32)

    def place_cells(place, index, base, count):
        targets, values = [], []
        for k in range(2):
            first = start_row(index + k) >> 7
            shift = start_col(index + k) & (LANES - 1)
            front, back = rows_of(place + 2 * k), rows_of(place + 2 * k + 1)
            for step, part in enumerate(
                (
                    jnp.where(across >= shift, front, 0.0),
                    back,
                    jnp.where(across >= shift, 0.0, front),
                )
            ):
                row = iota((count, tiles), 0) + base
                targets.append(jnp.where(first + step == row, 1.0, 0.0))
                values.append(part)
        return select_rows(jnp.concatenate(targets, axis=1), jnp.concatenate(values, axis=0))

    def lift(density):
        return CONTRAST * jax.nn.sigmoid(density)

    block = NX * 8
    sigma = jax.nn.sigmoid(place_cells(0, 0, 0, block))
    own = CONTRAST * sigma
    ahead = lift(place_cells(4, 2, 0, 16)[:8])
    behind = lift(place_cells(8, 4, block - 16, 16)[8:])
    targets = []
    for k in range(2):
        first = start_row(6 + k) >> 7
        last = start_row(8 + k) >> 7
        row = iota((48, tiles), 0)
        targets.append(
            jnp.where(
                (((first + 7) >> 3 == row) & (row < NX))
                | ((last >> 3) + NX == row)
                | (row >= 2 * NX),
                1.0,
                0.0,
            )
        )
    sides = lift(
        select_rows(
            jnp.concatenate(targets, axis=1), jnp.concatenate([rows_of(12), rows_of(13)], axis=0)
        )
    )

    def lanes_to(values, source):
        lane = iota(values.shape, 1)
        moved = pltpu.roll(values, (LOWER - source) % LANES, 1)
        return jnp.where((lane >= LOWER) & (lane < LOWER + LAYERS), moved, 0.0)

    grow[...] = jnp.zeros_like(grow)
    for quarter in range(4):
        source = quarter * LAYERS
        moved = lanes_to(own, source)
        for x in range(NX):
            grow[pl.ds((x + 2) * EY + quarter, 8, stride=4), :] = moved[8 * x : 8 * x + 8]
        grow[pl.ds((NX + 2) * EY + quarter, 8, stride=4), :] = lanes_to(ahead, source)
        grow[pl.ds(EY + quarter, 8, stride=4), :] = lanes_to(behind, source)
    grow[pl.ds(2 * EY + NY, NX, stride=EY), :] = lanes_to(sides[:NX], 0)
    grow[pl.ds(2 * EY + EY - 1, NX, stride=EY), :] = lanes_to(sides[NX : 2 * NX], 96)
    corner = sides[2 * NX : 2 * NX + 8]
    grow[pl.ds(EY + NY, 1), :] = lanes_to(corner, 32)[:1]
    grow[pl.ds((NX + 2) * EY + EY - 1, 1), :] = lanes_to(corner, 64)[:1]

    gx, gy = lax.axis_index("gx"), lax.axis_index("gy")
    low_x, high_x = gx > 0, gx < lax.axis_size("gx") - 1
    low_y, high_y = gy > 0, gy < lax.axis_size("gy") - 1
    y = iota((EY, LANES), 0)
    within = (y < NY) | ((y == NY) & high_y) | ((y == EY - 1) & low_y)


    for copy in copies[1:8]:
        copy.wait()
    flat_perm = perm_wide.reshape(EX * EY, LANES)
    for from_prev, beside, along, corner in ((True, before, below, low), (False, after, above, high)):
        row = EY - 1 if from_prev else NY
        flat_perm[pl.ds(2 * EY + row, NX, stride=EY), :] = beside[pl.ds(beside.shape[0] - NX, NX), :]
        perm_wide[1 if from_prev else NX + 2, :NY, :] = along[along.shape[0] - 1]
        for x in range(2):
            for other_row, at in ((EY - 1, (x + 1) * UP_ROWS - 1), (NY, 2 * UP_ROWS + (x + 1) * DOWN_ROWS - 1)):
                place = (0 if from_prev else NX + 2) + x
                perm_wide[place, other_row : other_row + 1, :] = corner[pl.ds(at, 1), :]

    def fill_halo(evolution):
        fields = wide[evolution]
        flat = fields.reshape(6 * EX * EY, LANES)
        for from_prev, beside, along in ((True, before, below), (False, after, above)):
            at = evolution * (beside.shape[0] // NX // 2)
            for field, comp, begin, count in plan_y(from_prev):
                for k in range(count):
                    row = EY + begin + k if from_prev else NY + begin + k
                    c = field * 3 + comp
                    flat[pl.ds((c * EX + 2) * EY + row, NX, stride=EY), :] = beside[pl.ds(at * NX, NX), :]
                    for corner, place in ((low, 0), (high, NX + 2)):
                        planes, start = (UP_ROWS, 0) if from_prev else (DOWN_ROWS, 2 * UP_ROWS)
                        for x in range(2):
                            fields[c, place + x, row : row + 1, :] = corner[pl.ds(start + at + x * planes, 1), :]
                    at += 1
            at = evolution * (along.shape[0] // 2)
            for field, comp, begin, count in plan(from_prev):
                for k in range(count):
                    place = begin + k + 2 if from_prev else NX + 2 + begin + k
                    fields[field * 3 + comp, place, :NY, :] = along[at]
                    at += 1

    cut = jnp.where((y < EY - 2) | low_y, COURANT, 0.0)

    for evolution in range(2):
        e, fields = 3 * evolution, wide[evolution]
        for copy in copies[8 + 2 * evolution : 10 + 2 * evolution]:
            copy.wait()
        fill_halo(evolution)
        for x in range(NX + 3):
            factor = cut if x >= 2 else jnp.where(low_x, cut, 0.0)
            here = [fields[c, x] for c in range(3)]
            curl = curl_e(here, [fields[c, x + 1] for c in (1, 2)])
            for c in range(3):
                turned[6 + e + c, x] = fields[3 + c, x] - factor * curl[c]
        for x in range(1, NX + 3):
            if e:
                scale = rate[x]
            else:
                eps = perm_wide[x] + grow[pl.ds(x * EY, EY), :]
                inside = within
                if x == 1:
                    inside = within & low_x
                if x == NX + 2:
                    inside = within & high_x
                scale = jnp.where(inside, COURANT / eps, 0.0)
                rate[x] = scale
            here = [turned[6 + e + c, x] for c in range(3)]
            curl = curl_h(here, [turned[6 + e + c, x - 1] for c in (1, 2)])
            for c in range(3):
                turned[e + c, x] = fields[c, x] + scale * curl[c]
    for x in range(1, NX + 2):
        factor = cut if x >= 2 else jnp.where(low_x, cut, 0.0)
        for e in (0, 3):
            here = [turned[e + c, x] for c in range(3)]
            curl = curl_e(here, [turned[e + c, x + 1] for c in (1, 2)])
            for c in range(3):
                wide[e // 3][3 + c, x] = turned[6 + e + c, x] - factor * curl[c]
    blend = math.cos(ANGULAR)
    for x in range(2, NX + 2):
        scale = rate[x]
        old, new = [], []
        for e in (0, 3):
            here = [wide[e // 3][3 + c, x] for c in range(3)]
            curl = curl_h(here, [wide[e // 3][3 + c, x - 1] for c in (1, 2)])
            old.append([turned[e + c, x][:NY] for c in range(3)])
            new.append([old[-1][c] + (scale * curl[c])[:NY] for c in range(3)])
        total = 0.0
        for c in range(3):
            final_v[c, x - 2] = new[0][c]
            total += old[0][c] * (old[1][c] + blend * new[1][c])
            total += new[0][c] * (new[1][c] + blend * old[1][c])
        overlap[pl.ds((x - 2) * NY, NY), :] = total
    final_copy.start()
    compact = jnp.zeros((block, LANES), F32)
    lane = iota((block, LANES), 1)
    for quarter in range(4):
        part = pltpu.roll(
            overlap[pl.ds(quarter, block, stride=4), :], (quarter * LAYERS - LOWER) % LANES, 1
        )
        compact = jnp.where(lane // LAYERS == quarter, part, compact)
    gradient = own * (1.0 - sigma) * compact
    picks, shifts = [], []
    for k in range(2):
        starts = start_col(k)
        shifts.append(starts & (LANES - 1))
        for step in range(3):
            picks.append(jnp.where(iota((tiles, block), 1) == (starts >> 7) + step, 1.0, 0.0))
    found = select_rows(jnp.concatenate(picks, axis=0), gradient)
    for k in range(2):
        head, back, tail = [found[(3 * k + i) * tiles : (3 * k + i + 1) * tiles] for i in range(3)]
        reply[pl.ds(2 * k, tiles, stride=4), :] = jnp.where(across >= shifts[k], head, tail)
        reply[pl.ds(2 * k + 1, tiles, stride=4), :] = back
    final_copy.wait()


def run_fields(ef, hf, ea, ha, perm, below, above, before, after, low, high, message):
    tiles = message.shape[0] // ROWS
    return pl.pallas_call(
        evolve,
        out_shape=(shape(3, NX, NY, LANES), shape(tiles * 4, LANES)),
        in_specs=[hbm()] * 5 + [anywhere()] * 7,
        out_specs=(hbm(), vmem()),
        scratch_shapes=[
            pltpu.VMEM((3, NX, NY, LANES), F32),
            pltpu.VMEM((6, EX, EY, LANES), F32),
            pltpu.VMEM((6, EX, EY, LANES), F32),
            pltpu.VMEM((EX, EY, LANES), F32),
            pltpu.VMEM((EX, EY, LANES), F32),
            pltpu.VMEM((EX * EY, LANES), F32),
            pltpu.VMEM((12, EX, EY, LANES), F32),
            pltpu.VMEM((NX * NY, LANES), F32),
            pltpu.VMEM(below.shape, F32),
            pltpu.VMEM(above.shape, F32),
            pltpu.VMEM(before.shape, F32),
            pltpu.VMEM(after.shape, F32),
            pltpu.VMEM(low.shape, F32),
            pltpu.VMEM(high.shape, F32),
            pltpu.VMEM(message.shape, F32),
            pltpu.SemaphoreType.DMA((13,)),
        ],
        compiler_params=params(50),
        cost_estimate=cost(8),
        name="evolve",
    )(ef, hf, ea, ha, perm, below, above, before, after, low, high, message)


def unpack_tiles(reply, match, out):
    tiles = out.shape[0]
    shift = match[:, 2 * tiles : 2 * tiles + 1].astype(jnp.int32)
    count = match[:, 2 * tiles + 1 : 2 * tiles + 2].astype(jnp.int32)
    rows = [
        jnp.concatenate(
            [reply[pl.ds(2 * k + half, tiles, stride=4), :] for half in range(2)], axis=1
        )
        for k in range(2)
    ]
    cells = select_rows(match[:, : 2 * tiles], jnp.concatenate(rows, axis=0))
    width = out.shape[1]
    for bit in range(7):
        cells = jnp.where((shift >> bit) & 1 == 1, pltpu.roll(cells, width - (1 << bit), 1), cells)
    out[...] = jnp.where(iota(out.shape, 1) < count, cells, 0.0)


def unpack(reply, match):
    tiles = match.shape[0]
    return pl.pallas_call(
        unpack_tiles,
        out_shape=shape(tiles, 2 * LANES),
        in_specs=[vmem()] * 2,
        out_specs=vmem(),
        compiler_params=params(16),
        cost_estimate=cost(2),
        name="unpack_tiles",
    )(reply, match)


def passed(block, axis, distance):
    devices = range(lax.axis_size(axis))
    return lax.ppermute(
        block, axis, [(i, i + distance) for i in devices if i + distance in devices]
    )


def exchange(block, depth):
    out = lax.all_to_all(
        block.reshape(-1, depth, LANES), ("gx", "gy"), split_axis=0, concat_axis=0, tiled=True
    )
    return out.reshape(block.shape)


def corner_rows(before, after, low, high):
    for out, first in ((low, NX - 2), (high, 0)):
        at = 0
        for src, planes in ((before, UP_ROWS), (after, DOWN_ROWS)):
            for x in range(2):
                out[pl.ds(at, planes), :] = src[pl.ds(first + x, planes, stride=NX), :]
                at += planes


def corners(before, after):
    rows = 2 * (UP_ROWS + DOWN_ROWS)
    return pl.pallas_call(
        corner_rows,
        out_shape=(shape(rows, LANES), shape(rows, LANES)),
        in_specs=[vmem()] * 2,
        out_specs=(vmem(), vmem()),
        compiler_params=params(16),
        cost_estimate=cost(20),
        name="corners",
    )(before, after)


def shards(ef, hf, ea, ha, perm, pattern, owners, tile_count, tile_start):
    up_x, down_x, up_y, down_y, message, match = prepare(
        ef, hf, ea, ha, perm, pattern, owners, tile_count, tile_start
    )
    arrived = exchange(message, 1)
    before, after = passed(up_y, "gy", 1), passed(down_y, "gy", -1)
    below, above = passed(up_x, "gx", 1), passed(down_x, "gx", -1)
    low, high = corners(before, after)
    low, high = passed(low, "gx", 1), passed(high, "gx", -1)
    final, reply = run_fields(
        ef, hf, ea, ha, perm, below, above, before, after, low, high, arrived
    )
    return final, unpack(exchange(reply, 4), match)


def solution(mesh):
    grid = P(None, "gx", "gy", None)
    tiles = ("gx", "gy")
    return jax.shard_map(
        shards,
        mesh=mesh,
        in_specs=(grid,) * 4 + (P("gx", "gy", None), P(tiles, None), P(tiles, None), P(tiles), P(tiles)),
        out_specs=(grid, P(tiles, None)),
        check_vma=False,
    )
```

```python
import functools
import math

import jax
import jax.numpy as jnp
from jax import lax
from jax.experimental import pallas as pl
from jax.experimental.pallas import tpu as pltpu
from jax.sharding import PartitionSpec as P

F32 = jnp.float32
LANES = 128
LAYERS = 32
LOWER = 48
COURANT = 0.5
ANGULAR = 0.9
CONTRAST = 8.0
EXACT = lax.Precision.HIGHEST

NX, NY = 16, 32
EX, EY = 20, 40
UP_ROWS = 23
DOWN_ROWS = 17
UP_X = 17
DOWN_X = 11
BESIDE = (EY - 1, NY, EY - 2)
TALL = NY + len(BESIDE)
ROWS = 15


def iota(shape, dim):
    return lax.broadcasted_iota(jnp.int32, shape, dim)


def params(limit):
    return pltpu.CompilerParams(vmem_limit_bytes=limit * 2**20)


def cost(micros):
    return pl.CostEstimate(flops=micros * 10**9, bytes_accessed=0, transcendentals=0)


def vmem():
    return pl.BlockSpec(memory_space=pltpu.VMEM)


def anywhere():
    return pl.BlockSpec(memory_space=pl.ANY)


def hbm():
    return pl.BlockSpec(memory_space=pltpu.HBM)


def shape(*dims):
    return jax.ShapeDtypeStruct(dims, F32)


def select_rows(marks, values):
    width = values.shape[1]
    high = values.astype(jnp.bfloat16)
    low = (values - high.astype(F32)).astype(jnp.bfloat16)
    found = jnp.dot(
        marks.astype(jnp.bfloat16),
        jnp.concatenate([high, low], axis=1),
        preferred_element_type=F32,
    )
    return found[:, :width] + found[:, width:]


def plan_y(to_next):
    if to_next:
        return [(0, 0, -2, 2), (0, 1, -2, 2), (0, 2, -2, 2), (1, 0, -2, 2), (1, 1, -1, 1), (1, 2, -2, 2)]
    return [(0, 0, 0, 2), (0, 1, 0, 1), (0, 2, 0, 2), (1, 0, 0, 1), (1, 1, 0, 1), (1, 2, 0, 1)]


def pack_tiles(pattern, owner, count, start, message, match):
    tiles = pattern.shape[0]
    square = (tiles, tiles)
    down, across = iota(square, 0), iota(square, 1)
    eye = down == across

    def column(row):
        return jnp.sum(jnp.where(eye, row.astype(F32), 0.0), axis=1, keepdims=True)

    owner_row = owner[...].astype(F32)
    owner_col = column(owner[...])
    same = owner_col == owner_row
    rank_row = jnp.sum(jnp.where(same & (down < across), 1.0, 0.0), axis=0, keepdims=True)
    rank_col = jnp.sum(jnp.where(same & (across < down), 1.0, 0.0), axis=1, keepdims=True)
    down_f, across_f = down.astype(F32), across.astype(F32)
    for k in range(2):
        match[:, k * tiles : (k + 1) * tiles] = jnp.where(
            (owner_col == across_f) & (rank_col == k), 1.0, 0.0
        )
    starts = column(start[...]).astype(jnp.int32)
    counts = column(count[...]).astype(jnp.int32)
    shift = starts & (LANES - 1)
    first = starts >> 7
    phase = first & 7
    match[:, 2 * tiles :] = jnp.where(
        across == 0, shift.astype(F32), jnp.where(across == 1, counts.astype(F32), 0.0)
    )
    wide = iota(pattern.shape, 1)
    cells = jnp.where(wide < counts, pattern[...], 0.0)
    for bit in range(7):
        cells = jnp.where((shift >> bit) & 1 == 1, pltpu.roll(cells, 1 << bit, 1), cells)
    front, back = cells[:, :LANES], cells[:, LANES:]
    head = jnp.where(across >= shift, front, 0.0)
    tail = jnp.where(across >= shift, 0.0, front)

    def pick(a, b, c):
        return jnp.where(
            phase == a, head, jnp.where(phase == b, back, jnp.where(phase == c, tail, 0.0))
        )

    low_y = pick(0, 7, 6)
    high_y = pick(7, 6, 5)
    low_corner = pltpu.roll(jnp.where((first + 7) >> 3 == NX - 1, low_y, 0.0), 32, 1)
    high_corner = pltpu.roll(jnp.where(first >> 3 == 0, high_y, 0.0), 96, 1)
    edges = jnp.where(
        across < 32,
        low_y,
        jnp.where(across < 64, low_corner, jnp.where(across < 96, high_corner, high_y)),
    )
    origin = jnp.broadcast_to(starts.astype(F32), square)
    everything = jnp.concatenate([front, back, edges, origin], axis=1)
    meta = jnp.zeros(square, F32)
    choose = [jnp.where((owner_row == down_f) & (rank_row == k), 1.0, 0.0) for k in range(2)]
    every_slot = select_rows(jnp.concatenate(choose, axis=0), everything)
    for k in range(2):
        slots = every_slot[k * tiles : (k + 1) * tiles]
        pair = slots[:, : 2 * LANES]
        edge = slots[:, 2 * LANES : 3 * LANES]
        origins = slots[:, 3 * LANES :]

        def other(values, distance):
            return pltpu.roll(values, -distance % tiles, 0)

        for place, distance in ((0, 0), (4, 8), (8, -8)):
            rows = other(pair, distance) if distance else pair
            for half in range(2):
                message[pl.ds(place + 2 * k + half, tiles, stride=ROWS), :] = rows[
                    :, half * LANES : (half + 1) * LANES
                ]
        message[pl.ds(12 + k, tiles, stride=ROWS), :] = jnp.where(
            across < 32,
            other(edge, 1),
            jnp.where(across < 64, other(edge, -7), jnp.where(across < 96, other(edge, 7), other(edge, -1))),
        )
        for place, distance in enumerate((0, 8, -8, 1, -1)):
            moved = other(origins, distance) if distance else origins
            meta = jnp.where(across == 2 * place + k, moved, meta)
    message[pl.ds(14, tiles, stride=ROWS), :] = meta


def prepare_all(
    ef, hf, ea, ha, perm, pattern_hbm, owner_hbm, count_hbm, start_hbm,
    first_x, last_x, first_x_perm, last_x_perm, up_y, down_y, message, match,
    first, last, first_perm, last_perm,
    pattern, owner, count, start, sems,
):
    small = [(owner_hbm, owner), (count_hbm, count), (start_hbm, start), (pattern_hbm, pattern)]
    loads_x, loads_y = [], []
    for begin, out, out_perm in ((NX - 2, last_x, last_x_perm), (0, first_x, first_x_perm)):
        for i, src in enumerate((ef, ea, hf, ha)):
            loads_x.append((src.at[:, pl.ds(begin, 2)], out.at[pl.ds(3 * i, 3)]))
        loads_x.append((perm.at[pl.ds(begin, 2)], out_perm))
    for dest, dest_perm, low in ((first, first_perm, 0), (last, last_perm, NY - 8)):
        rows = pl.ds(low, 8)
        for i, src in enumerate((ef, ea, hf, ha)):
            loads_y.append((src.at[:, :, rows], dest.at[pl.ds(3 * i, 3)]))
        loads_y.append((perm.at[:, rows], dest_perm))
    copies = [
        pltpu.make_async_copy(a, b, sems.at[i]) for i, (a, b) in enumerate(small + loads_y + loads_x)
    ]
    for copy in copies:
        copy.start()
    for copy in copies[:4]:
        copy.wait()
    pack_tiles(pattern, owner, count, start, message, match)
    for copy in copies[4:]:
        copy.wait()
    for to_next, src, src_perm, out in ((True, last, last_perm, up_y), (False, first, first_perm, down_y)):
        flat = src.reshape(12 * NX * 8, LANES)
        flat_perm = src_perm.reshape(NX * 8, LANES)
        at = 0
        for evolution in range(2):
            for field, comp, begin, planes in plan_y(to_next):
                for k in range(planes):
                    row = (field * 6 + evolution * 3 + comp) * NX * 8 + (begin + k) % 8
                    out[pl.ds(at * NX, NX), :] = flat[pl.ds(row, NX, stride=8), :]
                    at += 1
        out[pl.ds(at * NX, NX), :] = flat_perm[pl.ds(7 if to_next else 0, NX, stride=8), :]


def prepare(ef, hf, ea, ha, perm, pattern, owners, tile_count, tile_start):
    tiles = pattern.shape[0]
    return pl.pallas_call(
        prepare_all,
        out_shape=(
            shape(12, 2, NY, LANES),
            shape(12, 2, NY, LANES),
            shape(2, NY, LANES),
            shape(2, NY, LANES),
            shape(UP_ROWS * NX, LANES),
            shape(DOWN_ROWS * NX, LANES),
            shape(tiles * ROWS, LANES),
            shape(tiles, 3 * tiles),
        ),
        in_specs=[hbm()] * 9,
        out_specs=(vmem(),) * 8,
        scratch_shapes=[
            pltpu.VMEM((12, NX, 8, LANES), F32),
            pltpu.VMEM((12, NX, 8, LANES), F32),
            pltpu.VMEM((NX, 8, LANES), F32),
            pltpu.VMEM((NX, 8, LANES), F32),
            pltpu.VMEM((tiles, 2 * LANES), F32),
            pltpu.VMEM((1, tiles), jnp.int32),
            pltpu.VMEM((1, tiles), jnp.int32),
            pltpu.VMEM((1, tiles), jnp.int32),
            pltpu.SemaphoreType.DMA((24,)),
        ],
        compiler_params=params(56),
        cost_estimate=cost(3),
        name="prepare",
    )(
        ef, hf, ea, ha, perm, pattern,
        owners.reshape(1, tiles), tile_count.reshape(1, tiles), tile_start.reshape(1, tiles),
    )


def after_y(values):
    return pltpu.roll(values, values.shape[0] - 1, 0)


def before_y(values):
    return pltpu.roll(values, 1, 0)


def after_z(values):
    return jnp.where(iota(values.shape, 1) == LANES - 1, 0.0, pltpu.roll(values, LANES - 1, 1))


def before_z(values):
    return jnp.where(iota(values.shape, 1) == 0, 0.0, pltpu.roll(values, 1, 1))


def curl_e(here, ahead):
    ex, ey, ez = here
    next_y, next_z = ahead
    return (
        (after_y(ez) - ez) - (after_z(ey) - ey),
        (after_z(ex) - ex) - (next_z - ez),
        (next_y - ey) - (after_y(ex) - ex),
    )


def curl_h(here, behind):
    hx, hy, hz = here
    last_y, last_z = behind
    return (
        (hz - before_y(hz)) - (hy - before_z(hy)),
        (hx - before_z(hx)) - (hz - last_z),
        (hy - last_y) - (hx - before_y(hx)),
    )


def evolve(
    ef, hf, ea, ha, perm, below, above, before, after, message,
    final, reply,
    final_v, forward, adjoint, perm_wide, rate, grow, turned, overlap, sems,
):
    wide = (forward, adjoint)
    pairs = []
    pairs.append((perm, perm_wide.at[pl.ds(2, NX), pl.ds(0, NY)]))
    for i, src in ((0, ef), (1, hf), (2, ea), (3, ha)):
        pairs.append((src, wide[i // 2].at[pl.ds(3 * (i % 2), 3), pl.ds(2, NX), pl.ds(0, NY)]))
    copies = [pltpu.make_async_copy(a, b, sems.at[i]) for i, (a, b) in enumerate(pairs)]
    for copy in copies:
        copy.start()
    final_copy = pltpu.make_async_copy(final_v, final, sems.at[5])
    tiles = message.shape[0] // ROWS
    square = (tiles, LANES)
    across = iota(square, 1)

    def rows_of(place):
        return message[pl.ds(place, tiles, stride=ROWS), :]

    meta = rows_of(14)
    meta_rows = meta.T

    def start_row(index):
        return meta_rows[index : index + 1, :].astype(jnp.int32)

    def start_col(index):
        return meta[:, index : index + 1].astype(jnp.int32)

    def place_cells(place, index, base, count):
        targets, values = [], []
        for k in range(2):
            first = start_row(index + k) >> 7
            shift = start_col(index + k) & (LANES - 1)
            front, back = rows_of(place + 2 * k), rows_of(place + 2 * k + 1)
            for step, part in enumerate(
                (
                    jnp.where(across >= shift, front, 0.0),
                    back,
                    jnp.where(across >= shift, 0.0, front),
                )
            ):
                row = iota((count, tiles), 0) + base
                targets.append(jnp.where(first + step == row, 1.0, 0.0))
                values.append(part)
        return select_rows(jnp.concatenate(targets, axis=1), jnp.concatenate(values, axis=0))

    def lift(density):
        return CONTRAST * jax.nn.sigmoid(density)

    block = NX * 8
    sigma = jax.nn.sigmoid(place_cells(0, 0, 0, block))
    own = CONTRAST * sigma
    ahead = lift(place_cells(4, 2, 0, 16)[:8])
    behind = lift(place_cells(8, 4, block - 16, 16)[8:])
    targets = []
    for k in range(2):
        first = start_row(6 + k) >> 7
        last = start_row(8 + k) >> 7
        row = iota((48, tiles), 0)
        targets.append(
            jnp.where(
                (((first + 7) >> 3 == row) & (row < NX))
                | ((last >> 3) + NX == row)
                | (row >= 2 * NX),
                1.0,
                0.0,
            )
        )
    sides = lift(
        select_rows(
            jnp.concatenate(targets, axis=1), jnp.concatenate([rows_of(12), rows_of(13)], axis=0)
        )
    )

    def lanes_to(values, source):
        lane = iota(values.shape, 1)
        moved = pltpu.roll(values, (LOWER - source) % LANES, 1)
        return jnp.where((lane >= LOWER) & (lane < LOWER + LAYERS), moved, 0.0)

    grow[...] = jnp.zeros_like(grow)
    for quarter in range(4):
        source = quarter * LAYERS
        moved = lanes_to(own, source)
        for x in range(NX):
            grow[pl.ds((x + 2) * EY + quarter, 8, stride=4), :] = moved[8 * x : 8 * x + 8]
        grow[pl.ds((NX + 2) * EY + quarter, 8, stride=4), :] = lanes_to(ahead, source)
        grow[pl.ds(EY + quarter, 8, stride=4), :] = lanes_to(behind, source)
    grow[pl.ds(2 * EY + NY, NX, stride=EY), :] = lanes_to(sides[:NX], 0)
    grow[pl.ds(2 * EY + EY - 1, NX, stride=EY), :] = lanes_to(sides[NX : 2 * NX], 96)
    corner = sides[2 * NX : 2 * NX + 8]
    grow[pl.ds(EY + NY, 1), :] = lanes_to(corner, 32)[:1]
    grow[pl.ds((NX + 2) * EY + EY - 1, 1), :] = lanes_to(corner, 64)[:1]

    gx, gy = lax.axis_index("gx"), lax.axis_index("gy")
    low_x, high_x = gx > 0, gx < lax.axis_size("gx") - 1
    low_y, high_y = gy > 0, gy < lax.axis_size("gy") - 1
    y = iota((EY, LANES), 0)
    within = (y < NY) | ((y == NY) & high_y) | ((y == EY - 1) & low_y)


    copies[0].wait()
    flat_perm = perm_wide.reshape(EX * EY, LANES)
    for from_prev, beside, along in ((True, before, below), (False, after, above)):
        row = EY - 1 if from_prev else NY
        flat_perm[pl.ds(2 * EY + row, NX, stride=EY), :] = beside[pl.ds(beside.shape[0] - NX, NX), :]

    def take_plane(src, planes, at, dest):
        dest[:NY, :] = src[at * NY : (at + 1) * NY]
        for k, row in enumerate(BESIDE):
            dest[row : row + 1, :] = src[planes * NY + 3 * at + k : planes * NY + 3 * at + k + 1]

    take_plane(below, UP_X, UP_X - 1, perm_wide.at[1])
    take_plane(above, DOWN_X, DOWN_X - 1, perm_wide.at[NX + 2])

    def fill_halo(evolution):
        fields, h = wide[evolution], 6 + 3 * evolution
        flat = fields.reshape(6 * EX * EY, LANES)
        for from_prev, beside in ((True, before), (False, after)):
            at = evolution * (beside.shape[0] // NX // 2)
            for field, comp, begin, count in plan_y(from_prev):
                for k in range(count):
                    row = EY + begin + k if from_prev else NY + begin + k
                    c = field * 3 + comp
                    flat[pl.ds((c * EX + 2) * EY + row, NX, stride=EY), :] = beside[pl.ds(at * NX, NX), :]
                    at += 1
        places = [(fields, c, 1) for c in range(3)] + [(turned, h + c, 1) for c in range(3)]
        places += [(turned, h + c, 0) for c in (1, 2)]
        for i, (ref, c, x) in enumerate(places):
            take_plane(below, UP_X, 8 * evolution + i, ref.at[c, x])
        places = [(fields, c, NX + 2) for c in (1, 2)] + [(turned, h + c, NX + 2) for c in range(3)]
        for i, (ref, c, x) in enumerate(places):
            take_plane(above, DOWN_X, 5 * evolution + i, ref.at[c, x])

    cut = jnp.where((y < EY - 2) | low_y, COURANT, 0.0)

    for evolution in range(2):
        e, fields = 3 * evolution, wide[evolution]
        for copy in copies[1 + 2 * evolution : 3 + 2 * evolution]:
            copy.wait()
        fill_halo(evolution)
        edge_cut = jnp.where(low_x, cut, 0.0)
        turned[7 + e, 1] = turned[7 + e, 1] + edge_cut * fields[2, 2]
        turned[8 + e, 1] = turned[8 + e, 1] - edge_cut * fields[1, 2]
        for x in range(2, NX + 2):
            here = [fields[c, x] for c in range(3)]
            curl = curl_e(here, [fields[c, x + 1] for c in (1, 2)])
            for c in range(3):
                turned[6 + e + c, x] = fields[3 + c, x] - cut * curl[c]
        for x in range(1, NX + 3):
            if e:
                scale = rate[x]
            else:
                eps = perm_wide[x] + grow[pl.ds(x * EY, EY), :]
                inside = within
                if x == 1:
                    inside = within & low_x
                if x == NX + 2:
                    inside = within & high_x
                scale = jnp.where(inside, COURANT / eps, 0.0)
                rate[x] = scale
            here = [turned[6 + e + c, x] for c in range(3)]
            curl = curl_h(here, [turned[6 + e + c, x - 1] for c in (1, 2)])
            for c in range(1 if x == NX + 2 else 0, 3):
                turned[e + c, x] = fields[c, x] + scale * curl[c]
    for x in range(1, NX + 2):
        factor = cut if x >= 2 else jnp.where(low_x, cut, 0.0)
        for e in (0, 3):
            here = [turned[e + c, x] for c in range(3)]
            curl = curl_e(here, [turned[e + c, x + 1] for c in (1, 2)])
            for c in range(3):
                wide[e // 3][3 + c, x] = turned[6 + e + c, x] - factor * curl[c]
    blend = math.cos(ANGULAR)
    for x in range(2, NX + 2):
        scale = rate[x]
        old, new = [], []
        for e in (0, 3):
            here = [wide[e // 3][3 + c, x] for c in range(3)]
            curl = curl_h(here, [wide[e // 3][3 + c, x - 1] for c in (1, 2)])
            old.append([turned[e + c, x][:NY] for c in range(3)])
            new.append([old[-1][c] + (scale * curl[c])[:NY] for c in range(3)])
        total = 0.0
        for c in range(3):
            final_v[c, x - 2] = new[0][c]
            total += old[0][c] * (old[1][c] + blend * new[1][c])
            total += new[0][c] * (new[1][c] + blend * old[1][c])
        overlap[pl.ds((x - 2) * NY, NY), :] = total
    final_copy.start()
    compact = jnp.zeros((block, LANES), F32)
    lane = iota((block, LANES), 1)
    for quarter in range(4):
        part = pltpu.roll(
            overlap[pl.ds(quarter, block, stride=4), :], (quarter * LAYERS - LOWER) % LANES, 1
        )
        compact = jnp.where(lane // LAYERS == quarter, part, compact)
    gradient = own * (1.0 - sigma) * compact
    picks, shifts = [], []
    for k in range(2):
        starts = start_col(k)
        shifts.append(starts & (LANES - 1))
        for step in range(3):
            picks.append(jnp.where(iota((tiles, block), 1) == (starts >> 7) + step, 1.0, 0.0))
    found = select_rows(jnp.concatenate(picks, axis=0), gradient)
    for k in range(2):
        head, back, tail = [found[(3 * k + i) * tiles : (3 * k + i + 1) * tiles] for i in range(3)]
        reply[pl.ds(2 * k, tiles, stride=4), :] = jnp.where(across >= shifts[k], head, tail)
        reply[pl.ds(2 * k + 1, tiles, stride=4), :] = back
    final_copy.wait()


def run_fields(ef, hf, ea, ha, perm, below, above, before, after, message):
    tiles = message.shape[0] // ROWS
    return pl.pallas_call(
        evolve,
        out_shape=(shape(3, NX, NY, LANES), shape(tiles * 4, LANES)),
        in_specs=[hbm()] * 5 + [vmem()] * 5,
        out_specs=(hbm(), vmem()),
        scratch_shapes=[
            pltpu.VMEM((3, NX, NY, LANES), F32),
            pltpu.VMEM((6, EX, EY, LANES), F32),
            pltpu.VMEM((6, EX, EY, LANES), F32),
            pltpu.VMEM((EX, EY, LANES), F32),
            pltpu.VMEM((EX, EY, LANES), F32),
            pltpu.VMEM((EX * EY, LANES), F32),
            pltpu.VMEM((12, EX, EY, LANES), F32),
            pltpu.VMEM((NX * NY, LANES), F32),
            pltpu.SemaphoreType.DMA((6,)),
        ],
        compiler_params=params(51),
        cost_estimate=cost(8),
        name="evolve",
    )(ef, hf, ea, ha, perm, below, above, before, after, message)


def unpack_tiles(reply, match, out):
    tiles = out.shape[0]
    shift = match[:, 2 * tiles : 2 * tiles + 1].astype(jnp.int32)
    count = match[:, 2 * tiles + 1 : 2 * tiles + 2].astype(jnp.int32)
    rows = [
        jnp.concatenate(
            [reply[pl.ds(2 * k + half, tiles, stride=4), :] for half in range(2)], axis=1
        )
        for k in range(2)
    ]
    cells = select_rows(match[:, : 2 * tiles], jnp.concatenate(rows, axis=0))
    width = out.shape[1]
    for bit in range(7):
        cells = jnp.where((shift >> bit) & 1 == 1, pltpu.roll(cells, width - (1 << bit), 1), cells)
    out[...] = jnp.where(iota(out.shape, 1) < count, cells, 0.0)


def unpack(reply, match):
    tiles = match.shape[0]
    return pl.pallas_call(
        unpack_tiles,
        out_shape=shape(tiles, 2 * LANES),
        in_specs=[vmem()] * 2,
        out_specs=vmem(),
        compiler_params=params(16),
        cost_estimate=cost(2),
        name="unpack_tiles",
    )(reply, match)


def passed(block, axis, distance):
    devices = range(lax.axis_size(axis))
    return lax.ppermute(
        block, axis, [(i, i + distance) for i in devices if i + distance in devices]
    )


def exchange(block, depth):
    out = lax.all_to_all(
        block.reshape(-1, depth, LANES), ("gx", "gy"), split_axis=0, concat_axis=0, tiled=True
    )
    return out.reshape(block.shape)


def faces_x(first_x, last_x, first_perm, last_perm, before, after, up, down, tiles):
    places = (NX - 2, NX - 1, 0, 1)
    for from_prev, src in ((True, before), (False, after)):
        at = 0
        for evolution in range(2):
            for field, comp, begin, count in plan_y(from_prev):
                for k in range(count):
                    row = 8 + begin + k if from_prev else begin + k
                    for i, x in enumerate(places):
                        tiles[field * 6 + evolution * 3 + comp, i, row : row + 1, :] = src[
                            pl.ds(at * NX + x, 1), :
                        ]
                    at += 1

    def plane(c, i):
        block = last_x[c, i] if i < 2 else first_x[c, i - 2]
        return jnp.concatenate([block, tiles[c, i]], axis=0)

    def send(out, planes, at, values):
        out[at * NY : (at + 1) * NY] = values[:NY]
        for k, row in enumerate(BESIDE):
            out[planes * NY + 3 * at + k : planes * NY + 3 * at + k + 1] = values[row : row + 1]

    inside_y = lax.axis_index("gy") > 0
    rate = jnp.where((iota((EY, LANES), 0) < EY - 2) | inside_y, COURANT, 0.0)
    nothing = jnp.zeros((EY, LANES), F32)
    for evolution in range(2):
        e, h = 3 * evolution, 6 + 3 * evolution
        before_last, last, first, second = [[plane(e + c, i) for c in range(3)] for i in range(4)]
        curl = curl_e(before_last, last[1:])
        inner = [plane(h + c, 0) - rate * curl[c] for c in (1, 2)]
        curl = curl_e(last, [nothing, nothing])
        outer = [plane(h + c, 1) - rate * curl[c] for c in range(3)]
        for i, values in enumerate(last + outer + inner):
            send(up, UP_X, 8 * evolution + i, values)
        curl = curl_e(first, second[1:])
        outer = [plane(h + c, 2) - rate * curl[c] for c in range(3)]
        for i, values in enumerate(first[1:] + outer):
            send(down, DOWN_X, 5 * evolution + i, values)
    for out, planes, block, x in ((up, UP_X, last_perm[1], NX - 1), (down, DOWN_X, first_perm[0], 0)):
        at = planes - 1
        out[at * NY : (at + 1) * NY] = block
        for k, (src, rows) in enumerate(((before, UP_ROWS), (after, DOWN_ROWS))):
            out[planes * NY + 3 * at + k : planes * NY + 3 * at + k + 1] = src[pl.ds((rows - 1) * NX + x, 1), :]
        out[planes * TALL - 1 :] = jnp.zeros((1, LANES), F32)


def send_x(first_x, last_x, first_perm, last_perm, before, after):
    return pl.pallas_call(
        faces_x,
        out_shape=(shape(UP_X * TALL, LANES), shape(DOWN_X * TALL, LANES)),
        in_specs=[vmem()] * 6,
        out_specs=(vmem(), vmem()),
        scratch_shapes=[pltpu.VMEM((12, 4, 8, LANES), F32)],
        compiler_params=params(50),
        cost_estimate=cost(20),
        name="faces_x",
    )(first_x, last_x, first_perm, last_perm, before, after)


def shards(ef, hf, ea, ha, perm, pattern, owners, tile_count, tile_start):
    *edges, up_y, down_y, message, match = prepare(
        ef, hf, ea, ha, perm, pattern, owners, tile_count, tile_start
    )
    arrived = exchange(message, 1)
    before, after = passed(up_y, "gy", 1), passed(down_y, "gy", -1)
    up_x, down_x = send_x(*edges, before, after)
    below, above = passed(up_x, "gx", 1), passed(down_x, "gx", -1)
    final, reply = run_fields(
        ef, hf, ea, ha, perm, below, above, before, after, arrived
    )
    return final, unpack(exchange(reply, 4), match)


def solution(mesh):
    grid = P(None, "gx", "gy", None)
    tiles = ("gx", "gy")
    return jax.shard_map(
        shards,
        mesh=mesh,
        in_specs=(grid,) * 4 + (P("gx", "gy", None), P(tiles, None), P(tiles, None), P(tiles), P(tiles)),
        out_specs=(grid, P(tiles, None)),
        check_vma=False,
    )
```

```python
import functools
import math

import jax
import jax.numpy as jnp
from jax import lax
from jax.experimental import pallas as pl
from jax.experimental.pallas import tpu as pltpu
from jax.sharding import PartitionSpec as P

F32 = jnp.float32
LANES = 128
LAYERS = 32
LOWER = 48
COURANT = 0.5
ANGULAR = 0.9
CONTRAST = 8.0
EXACT = lax.Precision.HIGHEST

NX, NY = 16, 32
EY = 40
UP_ROWS = 23
DOWN_ROWS = 17
PLANES = 4
UP_X = 17
DOWN_X = 11
BESIDE = (EY - 1, NY, EY - 2)
TALL = NY + len(BESIDE)
ROWS = 11


def iota(shape, dim):
    return lax.broadcasted_iota(jnp.int32, shape, dim)


def params(limit):
    return pltpu.CompilerParams(vmem_limit_bytes=limit * 2**20)


def cost(micros):
    return pl.CostEstimate(flops=micros * 10**9, bytes_accessed=0, transcendentals=0)


def vmem():
    return pl.BlockSpec(memory_space=pltpu.VMEM)


def anywhere():
    return pl.BlockSpec(memory_space=pl.ANY)


def hbm():
    return pl.BlockSpec(memory_space=pltpu.HBM)


def shape(*dims):
    return jax.ShapeDtypeStruct(dims, F32)


def select_rows(marks, values):
    width = values.shape[1]
    high = values.astype(jnp.bfloat16)
    low = (values - high.astype(F32)).astype(jnp.bfloat16)
    found = jnp.dot(
        marks.astype(jnp.bfloat16),
        jnp.concatenate([high, low], axis=1),
        preferred_element_type=F32,
    )
    return found[:, :width] + found[:, width:]


def plan_y(to_next):
    if to_next:
        return [(0, 0, -2, 2), (0, 1, -2, 2), (0, 2, -2, 2), (1, 0, -2, 2), (1, 1, -1, 1), (1, 2, -2, 2)]
    return [(0, 0, 0, 2), (0, 1, 0, 1), (0, 2, 0, 2), (1, 0, 0, 1), (1, 1, 0, 1), (1, 2, 0, 1)]


def pack_tiles(pattern, owner, count, start, message, match):
    tiles = pattern.shape[0]
    square = (tiles, tiles)
    down, across = iota(square, 0), iota(square, 1)
    eye = down == across

    def column(row):
        return jnp.sum(jnp.where(eye, row.astype(F32), 0.0), axis=1, keepdims=True)

    owner_row = owner[...].astype(F32)
    owner_col = column(owner[...])
    same = owner_col == owner_row
    rank_row = jnp.sum(jnp.where(same & (down < across), 1.0, 0.0), axis=0, keepdims=True)
    rank_col = jnp.sum(jnp.where(same & (across < down), 1.0, 0.0), axis=1, keepdims=True)
    down_f, across_f = down.astype(F32), across.astype(F32)
    for k in range(2):
        match[:, k * tiles : (k + 1) * tiles] = jnp.where(
            (owner_col == across_f) & (rank_col == k), 1.0, 0.0
        )
    starts = column(start[...]).astype(jnp.int32)
    counts = column(count[...]).astype(jnp.int32)
    shift = starts & (LANES - 1)
    first = starts >> 7
    phase = first & 7
    match[:, 2 * tiles :] = jnp.where(
        across == 0, shift.astype(F32), jnp.where(across == 1, counts.astype(F32), 0.0)
    )
    wide = iota(pattern.shape, 1)
    cells = jnp.where(wide < counts, pattern[...], 0.0)
    for bit in range(7):
        cells = jnp.where((shift >> bit) & 1 == 1, pltpu.roll(cells, 1 << bit, 1), cells)
    front, back = cells[:, :LANES], cells[:, LANES:]
    head = jnp.where(across >= shift, front, 0.0)
    tail = jnp.where(across >= shift, 0.0, front)

    def pick(a, b, c):
        return jnp.where(
            phase == a, head, jnp.where(phase == b, back, jnp.where(phase == c, tail, 0.0))
        )

    low_y = pick(0, 7, 6)
    high_y = pick(7, 6, 5)
    low_corner = pltpu.roll(jnp.where((first + 7) >> 3 == NX - 1, low_y, 0.0), 32, 1)
    high_corner = pltpu.roll(jnp.where(first >> 3 == 0, high_y, 0.0), 96, 1)
    edges = jnp.where(
        across < 32,
        low_y,
        jnp.where(across < 64, low_corner, jnp.where(across < 96, high_corner, high_y)),
    )
    origin = jnp.broadcast_to(starts.astype(F32), square)
    everything = jnp.concatenate([front, back, edges, origin], axis=1)
    meta = jnp.zeros(square, F32)
    choose = [jnp.where((owner_row == down_f) & (rank_row == k), 1.0, 0.0) for k in range(2)]
    every_slot = select_rows(jnp.concatenate(choose, axis=0), everything)
    for k in range(2):
        slots = every_slot[k * tiles : (k + 1) * tiles]
        pair = slots[:, : 2 * LANES]
        edge = slots[:, 2 * LANES : 3 * LANES]
        origins = slots[:, 3 * LANES :]

        def other(values, distance):
            return pltpu.roll(values, -distance % tiles, 0)

        beyond = jnp.where(iota(pair.shape, 0) & 8 == 0, other(pair, -8), other(pair, 8))
        for place, rows in ((0, pair), (6, beyond)):
            for half in range(2):
                message[pl.ds(place + 2 * k + half, tiles, stride=ROWS), :] = rows[
                    :, half * LANES : (half + 1) * LANES
                ]
        message[pl.ds(4 + k, tiles, stride=ROWS), :] = jnp.where(
            across < 32,
            other(edge, 1),
            jnp.where(across < 64, other(edge, -7), jnp.where(across < 96, other(edge, 7), other(edge, -1))),
        )
        outer_origins = jnp.where(down & 8 == 0, other(origins, -8), other(origins, 8))
        for place, moved in enumerate((origins, other(origins, 1), other(origins, -1), outer_origins)):
            meta = jnp.where(across == 2 * place + k, moved, meta)
    message[pl.ds(10, tiles, stride=ROWS), :] = meta


def prepare_all(
    ef, hf, ea, ha, perm, pattern_hbm, owner_hbm, count_hbm, start_hbm,
    inner_y, outer_y, message, match,
    first, last, first_perm, last_perm,
    pattern, owner, count, start, sems,
):
    small = [(owner_hbm, owner), (count_hbm, count), (start_hbm, start), (pattern_hbm, pattern)]
    loads_y = []
    for dest, dest_perm, low in ((first, first_perm, 0), (last, last_perm, NY - 8)):
        rows = pl.ds(low, 8)
        for i, src in enumerate((ef, ea, hf, ha)):
            loads_y.append((src.at[:, :, rows], dest.at[pl.ds(3 * i, 3)]))
        loads_y.append((perm.at[:, rows], dest_perm))
    copies = [
        pltpu.make_async_copy(a, b, sems.at[i]) for i, (a, b) in enumerate(small + loads_y)
    ]
    for copy in copies:
        copy.start()
    for copy in copies[:4]:
        copy.wait()
    pack_tiles(pattern, owner, count, start, message, match)
    for copy in copies[4:]:
        copy.wait()

    def fill(up, down):
        for to_next, src, src_perm, out in ((True, last, last_perm, up), (False, first, first_perm, down)):
            flat = src.reshape(12 * NX * 8, LANES)
            flat_perm = src_perm.reshape(NX * 8, LANES)
            at = 0
            for evolution in range(2):
                for field, comp, begin, planes in plan_y(to_next):
                    for k in range(planes):
                        row = (field * 6 + evolution * 3 + comp) * NX * 8 + (begin + k) % 8
                        out[pl.ds(at * NX, NX), :] = flat[pl.ds(row, NX, stride=8), :]
                        at += 1
            out[pl.ds(at * NX, NX), :] = flat_perm[pl.ds(7 if to_next else 0, NX, stride=8), :]
        down[DOWN_ROWS * NX :] = jnp.zeros(((UP_ROWS - DOWN_ROWS) * NX, LANES), F32)

    to_pairs("gy", fill, inner_y, outer_y)


def prepare(ef, hf, ea, ha, perm, pattern, owners, tile_count, tile_start):
    tiles = pattern.shape[0]
    return pl.pallas_call(
        prepare_all,
        out_shape=(
            shape(UP_ROWS * NX, LANES),
            shape(UP_ROWS * NX, LANES),
            shape(tiles * ROWS, LANES),
            shape(tiles, 3 * tiles),
        ),
        in_specs=[hbm()] * 9,
        out_specs=(vmem(),) * 4,
        scratch_shapes=[
            pltpu.VMEM((12, NX, 8, LANES), F32),
            pltpu.VMEM((12, NX, 8, LANES), F32),
            pltpu.VMEM((NX, 8, LANES), F32),
            pltpu.VMEM((NX, 8, LANES), F32),
            pltpu.VMEM((tiles, 2 * LANES), F32),
            pltpu.VMEM((1, tiles), jnp.int32),
            pltpu.VMEM((1, tiles), jnp.int32),
            pltpu.VMEM((1, tiles), jnp.int32),
            pltpu.SemaphoreType.DMA((14,)),
        ],
        compiler_params=params(56),
        cost_estimate=cost(3),
        name="prepare",
    )(
        ef, hf, ea, ha, perm, pattern,
        owners.reshape(1, tiles), tile_count.reshape(1, tiles), tile_start.reshape(1, tiles),
    )


def to_pairs(axis, fill, inner, outer):
    even = lax.axis_index(axis) % 2 == 0
    pl.when(even)(lambda: fill(inner, outer))
    pl.when(jnp.logical_not(even))(lambda: fill(outer, inner))


def from_pairs(axis, inner, outer):
    even = lax.axis_index(axis) % 2 == 0

    def rows(from_prev, begin, count):
        near, far = (outer, inner) if from_prev else (inner, outer)
        return jnp.where(even, near[pl.ds(begin, count), :], far[pl.ds(begin, count), :])

    return rows


def after_y(values):
    return pltpu.roll(values, values.shape[0] - 1, 0)


def before_y(values):
    return pltpu.roll(values, 1, 0)


def after_z(values):
    return jnp.where(iota(values.shape, 1) == LANES - 1, 0.0, pltpu.roll(values, LANES - 1, 1))


def before_z(values):
    return jnp.where(iota(values.shape, 1) == 0, 0.0, pltpu.roll(values, 1, 1))


def curl_e(here, ahead):
    ex, ey, ez = here
    next_y, next_z = ahead
    return (
        (after_y(ez) - ez) - (after_z(ey) - ey),
        (after_z(ex) - ex) - (next_z - ez),
        (next_y - ey) - (after_y(ex) - ex),
    )


def curl_h(here, behind):
    hx, hy, hz = here
    last_y, last_z = behind
    return (
        (hz - before_y(hz)) - (hy - before_z(hy)),
        (hx - before_z(hx)) - (hz - last_z),
        (hy - last_y) - (hx - before_y(hx)),
    )


def start_row(meta_rows, index):
    return meta_rows[index : index + 1, :].astype(jnp.int32)


def start_col(meta, index):
    return meta[:, index : index + 1].astype(jnp.int32)


def step_one(
    ef, hf, ea, ha, perm, inner_any, outer_any, inner_y_any, outer_y_any, message_any,
    final, overlap, sigma_out, state, inner_out,
    forward, adjoint, perm_wide, grow, e_out, h_out, turned, rate, final_v, outer_local,
    inner, outer, inner_y, outer_y, message, sems,
):
    wide = (forward, adjoint)
    loads = [(src, wide[i // 2].at[pl.ds(3 * (i % 2), 3), :, pl.ds(0, NY)]) for i, src in enumerate((ef, hf, ea, ha))]
    pairs = [(message_any, message), (inner_y_any, inner_y), (outer_y_any, outer_y)]
    pairs += [(perm, perm_wide.at[:, pl.ds(0, NY)]), (inner_any, inner), (outer_any, outer)]
    pairs += loads
    copies = [pltpu.make_async_copy(a, b, sems.at[i]) for i, (a, b) in enumerate(pairs)]
    for copy in copies:
        copy.start()
    copies[0].wait()
    tiles = message.shape[0] // ROWS
    square = (tiles, LANES)
    across = iota(square, 1)
    block = NX * 8

    def rows_of(place):
        return message[pl.ds(place, tiles, stride=ROWS), :]

    meta = rows_of(10)
    meta_rows = meta.T
    even = lax.axis_index("gx") % 2 == 0

    def place_cells(place, index, row):
        targets, values = [], []
        for k in range(2):
            first = start_row(meta_rows, index + k) >> 7
            shift = start_col(meta, index + k) & (LANES - 1)
            front, back = rows_of(place + 2 * k), rows_of(place + 2 * k + 1)
            head, tail = jnp.where(across >= shift, front, 0.0), jnp.where(across >= shift, 0.0, front)
            for step, part in enumerate((head, back, tail)):
                targets.append(jnp.where(first + step == row, 1.0, 0.0))
                values.append(part)
        return select_rows(jnp.concatenate(targets, axis=1), jnp.concatenate(values, axis=0))

    density = place_cells(0, 0, iota((block, tiles), 0))
    beyond = place_cells(6, 6, iota((16, tiles), 0) + jnp.where(even, block - 8, 0))[:8]
    sigma = jax.nn.sigmoid(density)
    sigma_out[...] = sigma
    own = CONTRAST * sigma
    targets = []
    row = iota((3 * NX, tiles), 0)
    for k in range(2):
        first = start_row(meta_rows, 2 + k) >> 7
        last = start_row(meta_rows, 4 + k) >> 7
        targets.append(
            jnp.where(
                (((first + 7) >> 3 == row) & (row < NX))
                | ((last >> 3) + NX == row)
                | (row >= 2 * NX),
                1.0,
                0.0,
            )
        )
    sides = CONTRAST * jax.nn.sigmoid(
        select_rows(jnp.concatenate(targets, axis=1), jnp.concatenate([rows_of(4), rows_of(5)], axis=0))
    )

    def lanes_to(values, source):
        lane = iota(values.shape, 1)
        moved = pltpu.roll(values, (LOWER - source) % LANES, 1)
        return jnp.where((lane >= LOWER) & (lane < LOWER + LAYERS), moved, 0.0)

    for quarter in range(4):
        moved = lanes_to(own, quarter * LAYERS)
        for x in range(NX):
            grow[pl.ds(x * EY + quarter, 8, stride=4), :] = moved[8 * x : 8 * x + 8]
    grow[pl.ds(NY, NX, stride=EY), :] = lanes_to(sides[:NX], 0)
    grow[pl.ds(EY - 1, NX, stride=EY), :] = lanes_to(sides[NX : 2 * NX], 96)
    beyond = CONTRAST * jax.nn.sigmoid(beyond)
    for quarter in range(4):
        grow[pl.ds(NX * EY + quarter, 8, stride=4), :] = lanes_to(beyond, quarter * LAYERS)
    corner = sides[2 * NX : 2 * NX + 8]
    grow[pl.ds(NX * EY + NY, 1), :] = lanes_to(corner, 32)[:1]
    grow[pl.ds(NX * EY + EY - 1, 1), :] = lanes_to(corner, 64)[:1]

    low_x = lax.axis_index("gx") > 0
    gy = lax.axis_index("gy")
    low_y, high_y = gy > 0, gy < lax.axis_size("gy") - 1
    y = iota((EY, LANES), 0)
    within = (y < NY) | ((y == NY) & high_y) | ((y == EY - 1) & low_y)
    cut = jnp.where((y < EY - 2) | low_y, COURANT, 0.0)
    edge_cut = jnp.where(low_x, cut, 0.0)
    nothing = jnp.zeros((EY, LANES), F32)
    for copy in copies[1:6]:
        copy.wait()
    flat_perm = perm_wide.reshape(NX * EY, LANES)
    beside_y = from_pairs("gy", inner_y, outer_y)
    flat_perm[pl.ds(EY - 1, NX, stride=EY), :] = beside_y(True, (UP_ROWS - 1) * NX, NX)
    flat_perm[pl.ds(NY, NX, stride=EY), :] = beside_y(False, (DOWN_ROWS - 1) * NX, NX)

    def halo_plane(src, planes, at):
        begin, row = planes * NY + 3 * at, iota((8, LANES), 0)
        tile = nothing[:8]
        for k in range(3):
            tile = jnp.where(row == BESIDE[k] - NY, src[begin + k : begin + k + 1], tile)
        return jnp.concatenate([src[at * NY : (at + 1) * NY], tile], axis=0)

    def e_ahead(evolution, c):
        return jnp.where(
            even,
            halo_plane(inner, PLANES, 2 * evolution + c - 1),
            halo_plane(outer, DOWN_X, 5 * evolution + c - 1),
        )

    def h_behind(evolution, c):
        return jnp.where(
            even,
            halo_plane(outer, UP_X, 8 * evolution + 3 + c),
            halo_plane(inner, PLANES, 2 * evolution + c - 1),
        )

    for evolution in range(2):
        e, fields = 3 * evolution, wide[evolution]
        for copy in copies[6 + 2 * evolution : 8 + 2 * evolution]:
            copy.wait()
        flat = fields.reshape(6 * NX * EY, LANES)
        for from_prev, planes in ((True, UP_ROWS), (False, DOWN_ROWS)):
            at = evolution * (planes // 2)
            for field, comp, begin, count in plan_y(from_prev):
                for k in range(count):
                    row = EY + begin + k if from_prev else NY + begin + k
                    place = (field * 3 + comp) * NX * EY + row
                    flat[pl.ds(place, NX, stride=EY), :] = beside_y(from_prev, at * NX, NX)
                    at += 1
        for x in range(NX):
            here = [fields[c, x] for c in range(3)]
            if x < NX - 1:
                ahead = [fields[c, x + 1] for c in (1, 2)]
            else:
                ahead = [e_ahead(evolution, c) for c in (1, 2)]
            curl = curl_e(here, ahead)
            for c in range(3):
                h_out[e + c, x] = fields[3 + c, x] - cut * curl[c]
        for x in range(NX):
            if evolution:
                scale = grow[pl.ds(x * EY, EY), :]
            else:
                eps = perm_wide[x] + grow[pl.ds(x * EY, EY), :]
                scale = jnp.where(within, COURANT / eps, 0.0)
                grow[pl.ds(x * EY, EY), :] = scale
                rate[x] = scale[:NY]
            here = [h_out[e + c, x] for c in range(3)]
            if x > 0:
                behind = [h_out[e + c, x - 1] for c in (1, 2)]
            else:
                behind = [
                    h_behind(evolution, 1) + edge_cut * fields[2, 0],
                    h_behind(evolution, 2) - edge_cut * fields[1, 0],
                ]
            curl = curl_h(here, behind)
            for c in range(3):
                e_out[e + c, x] = fields[c, x] + scale * curl[c]

    def outer_rate(planes, inside, rows):
        eps = halo_plane(outer, planes, planes - 1) + grow[pl.ds(NX * EY, EY), :]
        return jnp.where(rows & inside, COURANT / eps, 0.0)

    def put_up(out, evolution, h, e, factor):
        curl = curl_e(e, [nothing, nothing])
        for c in (1, 2):
            at = (2 * evolution + c - 1) * NY
            out[at : at + NY] = (h[c] - factor * curl[c])[:NY]

    def put_down(out, evolution, e_y, e_z):
        at = 2 * evolution * NY
        out[at : at + NY] = e_y[:NY]
        out[at + NY : at + 2 * NY] = e_z[:NY]
        at = PLANES * NY + evolution
        out[at : at + 1] = e_y[EY - 1 :]

    for out in (inner_out, outer_local):
        out[PLANES * NY :] = jnp.zeros((8, LANES), F32)

    def even_device():
        scale = outer_rate(UP_X, low_x, within & (y < EY - 1))
        for evolution in range(2):
            e = 3 * evolution
            last = [e_out[e + c, NX - 1] for c in range(3)]
            put_up(inner_out, evolution, [h_out[e + c, NX - 1] for c in range(3)], last, cut)
            electric, magnetic = [
                [halo_plane(outer, UP_X, 8 * evolution + i + c) for c in range(3)] for i in (0, 3)
            ]
            start = wide[evolution]
            magnetic[1] = magnetic[1] + edge_cut * start[2, 0]
            magnetic[2] = magnetic[2] - edge_cut * start[1, 0]
            curl = curl_h(magnetic, [halo_plane(outer, UP_X, 8 * evolution + 6 + c) for c in range(2)])
            electric = [electric[c] + scale * curl[c] for c in range(3)]
            put_up(outer_local, evolution, magnetic, electric, edge_cut)

    def odd_device():
        scale = outer_rate(DOWN_X, lax.axis_index("gx") < lax.axis_size("gx") - 1, within & (y != NY))
        for evolution in range(2):
            e = 3 * evolution
            put_down(inner_out, evolution, e_out[e + 1, 0], e_out[e + 2, 0])
            planes = [halo_plane(outer, DOWN_X, 5 * evolution + i) for i in range(5)]
            curl = curl_h(planes[2:], [h_out[e + c, NX - 1] for c in (1, 2)])
            put_down(outer_local, evolution, planes[0] + scale * curl[1], planes[1] + scale * curl[2])

    pl.when(even)(even_device)
    pl.when(jnp.logical_not(even))(odd_device)

    def ahead_plane(at, evolution):
        tile = jnp.where(iota((8, LANES), 0) == 7, outer_local[pl.ds(PLANES * NY + evolution, 1), :], 0.0)
        plane = jnp.concatenate([outer_local[pl.ds(at * NY, NY), :], tile], axis=0)
        return jnp.where(even, 0.0, plane)

    for x in range(NX):
        for evolution in range(2):
            e = 3 * evolution
            here = [e_out[e + c, x] for c in range(3)]
            if x < NX - 1:
                ahead = [e_out[e + c, x + 1] for c in (1, 2)]
            else:
                ahead = [ahead_plane(2 * evolution + c, evolution) for c in range(2)]
            curl = curl_e(here, ahead)
            for c in range(3):
                turned[e + c, x] = h_out[e + c, x] - cut * curl[c]
    leaving = []
    for x in range(NX):
        old, new = [], []
        for evolution in range(2):
            e = 3 * evolution
            if x > 0:
                behind = [turned[e + c, x - 1][:NY] for c in (1, 2)]
            else:
                at = 2 * evolution * NY
                factor = edge_cut[:NY]
                behind = [
                    outer_local[pl.ds(at, NY), :] + factor * e_out[e + 2, 0][:NY],
                    outer_local[pl.ds(at + NY, NY), :] - factor * e_out[e + 1, 0][:NY],
                ]
            old.append([e_out[e + c, x][:NY] for c in range(3)])
            new.append(last_e(old[-1], rate[x], [turned[e + c, x] for c in range(3)], behind))
        for c in range(3):
            final_v[c, x] = new[0][c]
        overlap[pl.ds(x * NY, NY), :] = product(old, new)
        if x % 4 == 3:
            part = pl.ds(x - 3, 4)
            leaving.append(pltpu.make_async_copy(final_v.at[:, part], final.at[:, part], sems.at[10 + x // 4]))
            leaving[-1].start()

    def keep(x):
        for c in range(6):
            state[c] = e_out[c, x]
            state[6 + c] = turned[c, x]
        for evolution in range(2):
            for c in (1, 2):
                state[11 + 2 * evolution + c] = turned[3 * evolution + c, NX - 2]
        state[16, :NY] = rate[x]
        state[16, NY:] = nothing[NY:]

    pl.when(even)(lambda: keep(NX - 1))
    pl.when(jnp.logical_not(even))(lambda: keep(0))
    for copy in leaving:
        copy.wait()


def last_e(electric, scale, magnetic, behind):
    last_x, last_z = before_y(magnetic[0])[:NY], before_y(magnetic[2])[:NY]
    hx, hy, hz = [v[:NY] for v in magnetic]
    curl = (
        (hz - last_z) - (hy - before_z(hy)),
        (hx - before_z(hx)) - (hz - behind[1]),
        (hy - behind[0]) - (hx - last_x),
    )
    return [electric[c] + scale * curl[c] for c in range(3)]


def product(old, new):
    blend = math.cos(ANGULAR)
    total = 0.0
    for c in range(3):
        total += old[0][c] * (old[1][c] + blend * new[1][c])
        total += new[0][c] * (new[1][c] + blend * old[1][c])
    return total


def first_step(ef, hf, ea, ha, perm, inner, outer, inner_y, outer_y, message):
    return pl.pallas_call(
        step_one,
        out_shape=(
            shape(3, NX, NY, LANES),
            shape(NX * NY, LANES),
            shape(NX * 8, LANES),
            shape(17, EY, LANES),
            shape(PLANES * NY + 8, LANES),
        ),
        in_specs=[hbm()] * 5 + [anywhere()] * 5,
        out_specs=(hbm(),) + (vmem(),) * 4,
        scratch_shapes=[
            pltpu.VMEM((6, NX, EY, LANES), F32),
            pltpu.VMEM((6, NX, EY, LANES), F32),
            pltpu.VMEM((NX, EY, LANES), F32),
            pltpu.VMEM(((NX + 1) * EY, LANES), F32),
            pltpu.VMEM((6, NX, EY, LANES), F32),
            pltpu.VMEM((6, NX, EY, LANES), F32),
            pltpu.VMEM((6, NX, EY, LANES), F32),
            pltpu.VMEM((NX, NY, LANES), F32),
            pltpu.VMEM((3, NX, NY, LANES), F32),
            pltpu.VMEM((PLANES * NY + 8, LANES), F32),
            pltpu.VMEM(inner.shape, F32),
            pltpu.VMEM(outer.shape, F32),
            pltpu.VMEM(inner_y.shape, F32),
            pltpu.VMEM(outer_y.shape, F32),
            pltpu.VMEM(message.shape, F32),
            pltpu.SemaphoreType.DMA((14,)),
        ],
        compiler_params=params(51),
        cost_estimate=cost(5),
        name="step_one",
    )(ef, hf, ea, ha, perm, inner, outer, inner_y, outer_y, message)


def step_two(final_in, overlap_in, sigma_in, state, inner, message, final, reply, plane, overlap, sem):
    even = lax.axis_index("gx") % 2 == 0
    low_y = lax.axis_index("gy") > 0
    y = iota((EY, LANES), 0)
    cut = jnp.where(((y < EY - 2) | low_y) & even, COURANT, 0.0)
    x = jnp.where(even, NX - 1, 0)
    overlap[...] = overlap_in[...]
    old, new = [], []
    for evolution in range(2):
        e, at = 3 * evolution, 2 * evolution * NY
        rows = [inner[at + c * NY : at + (c + 1) * NY] for c in range(2)]
        beside = inner[PLANES * NY + evolution : PLANES * NY + evolution + 1]
        tile = jnp.where(iota((8, LANES), 0) == 7, beside, 0.0)
        ahead = [jnp.concatenate([r, tile], axis=0) for r in rows]
        old.append([state[e + c][:NY] for c in range(3)])
        magnetic = [state[6 + e], state[7 + e] + cut * ahead[1], state[8 + e] - cut * ahead[0]]
        behind = [
            jnp.where(even, state[12 + 2 * evolution][:NY], rows[0] + COURANT * old[-1][2]),
            jnp.where(even, state[13 + 2 * evolution][:NY], rows[1] - COURANT * old[-1][1]),
        ]
        new.append(last_e(old[-1], state[16][:NY], magnetic, behind))
    for c in range(3):
        plane[c] = new[0][c]
    final_copy = pltpu.make_async_copy(plane, final.at[:, x], sem)
    final_copy.start()
    overlap[pl.ds(pl.multiple_of(x * NY, NY), NY), :] = product(old, new)
    tiles = message.shape[0] // ROWS
    across = iota((tiles, LANES), 1)
    meta = message[pl.ds(10, tiles, stride=ROWS), :]
    block = NX * 8
    compact = jnp.zeros((block, LANES), F32)
    lane = iota((block, LANES), 1)
    for quarter in range(4):
        part = pltpu.roll(
            overlap[pl.ds(quarter, block, stride=4), :], (quarter * LAYERS - LOWER) % LANES, 1
        )
        compact = jnp.where(lane // LAYERS == quarter, part, compact)
    sigma = sigma_in[...]
    gradient = CONTRAST * sigma * (1.0 - sigma) * compact
    picks, shifts = [], []
    for k in range(2):
        starts = start_col(meta, k)
        shifts.append(starts & (LANES - 1))
        for step in range(3):
            picks.append(jnp.where(iota((tiles, block), 1) == (starts >> 7) + step, 1.0, 0.0))
    found = select_rows(jnp.concatenate(picks, axis=0), gradient)
    for k in range(2):
        head, back, tail = [found[(3 * k + i) * tiles : (3 * k + i + 1) * tiles] for i in range(3)]
        reply[pl.ds(2 * k, tiles, stride=4), :] = jnp.where(across >= shifts[k], head, tail)
        reply[pl.ds(2 * k + 1, tiles, stride=4), :] = back
    final_copy.wait()


def second_step(final, overlap, sigma, state, inner, message):
    tiles = message.shape[0] // ROWS
    return pl.pallas_call(
        step_two,
        out_shape=(shape(3, NX, NY, LANES), shape(tiles * 4, LANES)),
        in_specs=[hbm()] + [vmem()] * 5,
        out_specs=(hbm(), vmem()),
        input_output_aliases={0: 0},
        scratch_shapes=[
            pltpu.VMEM((3, NY, LANES), F32),
            pltpu.VMEM((NX * NY, LANES), F32),
            pltpu.SemaphoreType.DMA,
        ],
        compiler_params=params(30),
        cost_estimate=cost(1),
        name="step_two",
    )(final, overlap, sigma, state, inner, message)


def unpack_tiles(reply, match, out):
    tiles = out.shape[0]
    shift = match[:, 2 * tiles : 2 * tiles + 1].astype(jnp.int32)
    count = match[:, 2 * tiles + 1 : 2 * tiles + 2].astype(jnp.int32)
    rows = [
        jnp.concatenate(
            [reply[pl.ds(2 * k + half, tiles, stride=4), :] for half in range(2)], axis=1
        )
        for k in range(2)
    ]
    cells = select_rows(match[:, : 2 * tiles], jnp.concatenate(rows, axis=0))
    width = out.shape[1]
    for bit in range(7):
        cells = jnp.where((shift >> bit) & 1 == 1, pltpu.roll(cells, width - (1 << bit), 1), cells)
    out[...] = jnp.where(iota(out.shape, 1) < count, cells, 0.0)


def unpack(reply, match):
    tiles = match.shape[0]
    return pl.pallas_call(
        unpack_tiles,
        out_shape=shape(tiles, 2 * LANES),
        in_specs=[vmem()] * 2,
        out_specs=vmem(),
        compiler_params=params(16),
        cost_estimate=cost(2),
        name="unpack_tiles",
    )(reply, match)


def swapped(block, axis, first):
    pairs = [(i, i + 1) for i in range(first, lax.axis_size(axis) - 1, 2)]
    return lax.ppermute(block, axis, pairs + [(j, i) for i, j in pairs])


def exchange(block, depth):
    out = lax.all_to_all(
        block.reshape(-1, depth, LANES), ("gx", "gy"), split_axis=0, concat_axis=0, tiled=True
    )
    return out.reshape(block.shape)


def faces_x(ef, hf, ea, ha, perm, inner_y, outer_y, inner_out, outer_out, first_x, last_x, edge_perm, tiles, sems):
    pairs = []
    for i, src in enumerate((ef, ea, hf, ha)):
        pairs.append((src.at[:, pl.ds(NX - 2, 2)], last_x.at[pl.ds(3 * i, 3)]))
        pairs.append((src.at[:, pl.ds(0, 2)], first_x.at[pl.ds(3 * i, 3)]))
    pairs.append((perm.at[NX - 1], edge_perm.at[0]))
    pairs.append((perm.at[0], edge_perm.at[1]))
    copies = [pltpu.make_async_copy(a, b, sems.at[i]) for i, (a, b) in enumerate(pairs)]
    for copy in copies:
        copy.start()
    beside = from_pairs("gy", inner_y, outer_y)
    for from_prev in (True, False):
        at = 0
        for evolution in range(2):
            for field, comp, begin, count in plan_y(from_prev):
                for k in range(count):
                    row = 8 + begin + k if from_prev else begin + k
                    for i, x in enumerate((NX - 2, NX - 1, 0, 1)):
                        tiles[field * 6 + evolution * 3 + comp, i, row : row + 1, :] = beside(
                            from_prev, at * NX + x, 1
                        )
                    at += 1
    for copy in copies:
        copy.wait()

    def plane(c, i):
        block = last_x[c, i] if i < 2 else first_x[c, i - 2]
        return jnp.concatenate([block, tiles[c, i]], axis=0)

    def send(out, planes, at, values):
        out[at * NY : (at + 1) * NY] = values[:NY]
        for k, row in enumerate(BESIDE):
            out[planes * NY + 3 * at + k : planes * NY + 3 * at + k + 1] = values[row : row + 1]

    def send_perm(out, planes, i, x):
        at = planes - 1
        out[at * NY : (at + 1) * NY] = edge_perm[i]
        for k, (from_prev, count) in enumerate(((True, UP_ROWS), (False, DOWN_ROWS))):
            begin = planes * NY + 3 * at + k
            out[begin : begin + 1] = beside(from_prev, (count - 1) * NX + x, 1)
        out[planes * TALL - 1 :] = jnp.zeros((outer_out.shape[0] - planes * TALL + 1, LANES), F32)

    inside_y = lax.axis_index("gy") > 0
    rate = jnp.where((iota((EY, LANES), 0) < EY - 2) | inside_y, COURANT, 0.0)
    nothing = jnp.zeros((EY, LANES), F32)

    def even_device():
        for evolution in range(2):
            e, h = 3 * evolution, 6 + 3 * evolution
            curl = curl_e([plane(e + c, 1) for c in range(3)], [nothing, nothing])
            for c in (1, 2):
                send(inner_out, PLANES, 2 * evolution + c - 1, plane(h + c, 1) - rate * curl[c])
            first, second = [[plane(e + c, i) for c in range(3)] for i in (2, 3)]
            curl = curl_e(first, second[1:])
            planes = first[1:] + [plane(h + c, 2) - rate * curl[c] for c in range(3)]
            for i, values in enumerate(planes):
                send(outer_out, DOWN_X, 5 * evolution + i, values)
        send_perm(outer_out, DOWN_X, 1, 0)

    def odd_device():
        for evolution in range(2):
            e, h = 3 * evolution, 6 + 3 * evolution
            for c in (1, 2):
                send(inner_out, PLANES, 2 * evolution + c - 1, plane(e + c, 2))
            before_last, last = [[plane(e + c, i) for c in range(3)] for i in (0, 1)]
            curl = curl_e(before_last, last[1:])
            planes = [plane(h + c, 0) - rate * curl[c] for c in (1, 2)]
            curl = curl_e(last, [nothing, nothing])
            planes = last + [plane(h + c, 1) - rate * curl[c] for c in range(3)] + planes
            for i, values in enumerate(planes):
                send(outer_out, UP_X, 8 * evolution + i, values)
        send_perm(outer_out, UP_X, 0, NX - 1)

    even = lax.axis_index("gx") % 2 == 0
    pl.when(even)(even_device)
    pl.when(jnp.logical_not(even))(odd_device)


def send_x(ef, hf, ea, ha, perm, inner_y, outer_y):
    return pl.pallas_call(
        faces_x,
        out_shape=(shape(PLANES * TALL, LANES), shape(UP_X * TALL, LANES)),
        in_specs=[hbm()] * 5 + [vmem()] * 2,
        out_specs=(vmem(), vmem()),
        scratch_shapes=[
            pltpu.VMEM((12, 2, NY, LANES), F32),
            pltpu.VMEM((12, 2, NY, LANES), F32),
            pltpu.VMEM((2, NY, LANES), F32),
            pltpu.VMEM((12, 4, 8, LANES), F32),
            pltpu.SemaphoreType.DMA((10,)),
        ],
        compiler_params=params(50),
        cost_estimate=cost(20),
        name="faces_x",
    )(ef, hf, ea, ha, perm, inner_y, outer_y)


def shards(ef, hf, ea, ha, perm, pattern, owners, tile_count, tile_start):
    inner_y, outer_y, message, match = prepare(
        ef, hf, ea, ha, perm, pattern, owners, tile_count, tile_start
    )
    outer_y, inner_y = swapped(outer_y, "gy", 1), swapped(inner_y, "gy", 0)
    arrived = exchange(message, 1)
    inner, outer = send_x(ef, hf, ea, ha, perm, inner_y, outer_y)
    outer, inner = swapped(outer, "gx", 1), swapped(inner, "gx", 0)
    *state, inner = first_step(
        ef, hf, ea, ha, perm, inner, outer, inner_y, outer_y, arrived
    )
    final, reply = second_step(*state, swapped(inner, "gx", 0), arrived)
    return final, unpack(exchange(reply, 4), match)


def solution(mesh):
    grid = P(None, "gx", "gy", None)
    tiles = ("gx", "gy")
    return jax.shard_map(
        shards,
        mesh=mesh,
        in_specs=(grid,) * 4 + (P("gx", "gy", None), P(tiles, None), P(tiles, None), P(tiles), P(tiles)),
        out_specs=(grid, P(tiles, None)),
        check_vma=False,
    )
```

```python
import functools
import math

import jax
import jax.numpy as jnp
from jax import lax
from jax.experimental import pallas as pl
from jax.experimental.pallas import tpu as pltpu
from jax.sharding import PartitionSpec as P

F32 = jnp.float32
LANES = 128
LAYERS = 32
LOWER = 48
COURANT = 0.5
ANGULAR = 0.9
CONTRAST = 8.0
EXACT = lax.Precision.HIGHEST

NX, NY = 16, 32
EY = 40
UP_ROWS = 23
DOWN_ROWS = 17
PLANES = 4
UP_X = 17
DOWN_X = 11
BESIDE = (EY - 1, NY, EY - 2)
TALL = NY + len(BESIDE)
ROWS = 10
META = 64


def iota(shape, dim):
    return lax.broadcasted_iota(jnp.int32, shape, dim)


def params(limit):
    return pltpu.CompilerParams(vmem_limit_bytes=limit * 2**20)


def cost(micros):
    return pl.CostEstimate(flops=micros * 10**9, bytes_accessed=0, transcendentals=0)


def vmem():
    return pl.BlockSpec(memory_space=pltpu.VMEM)


def anywhere():
    return pl.BlockSpec(memory_space=pl.ANY)


def hbm():
    return pl.BlockSpec(memory_space=pltpu.HBM)


def shape(*dims):
    return jax.ShapeDtypeStruct(dims, F32)


def select_rows(marks, values):
    width = values.shape[1]
    high = values.astype(jnp.bfloat16)
    low = (values - high.astype(F32)).astype(jnp.bfloat16)
    found = jnp.dot(
        marks.astype(jnp.bfloat16),
        jnp.concatenate([high, low], axis=1),
        preferred_element_type=F32,
    )
    return found[:, :width] + found[:, width:]


def plan_y(to_next):
    if to_next:
        return [(0, 0, -2, 2), (0, 1, -2, 2), (0, 2, -2, 2), (1, 0, -2, 2), (1, 1, -1, 1), (1, 2, -2, 2)]
    return [(0, 0, 0, 2), (0, 1, 0, 1), (0, 2, 0, 2), (1, 0, 0, 1), (1, 1, 0, 1), (1, 2, 0, 1)]


def pack_tiles(pattern, owner, count, start, message, match):
    tiles = pattern.shape[0]
    square = (tiles, tiles)
    down, across = iota(square, 0), iota(square, 1)
    eye = down == across

    def column(row):
        return jnp.sum(jnp.where(eye, row.astype(F32), 0.0), axis=1, keepdims=True)

    owner_row = owner[...].astype(F32)
    owner_col = column(owner[...])
    same = owner_col == owner_row
    rank_row = jnp.sum(jnp.where(same & (down < across), 1.0, 0.0), axis=0, keepdims=True)
    rank_col = jnp.sum(jnp.where(same & (across < down), 1.0, 0.0), axis=1, keepdims=True)
    down_f, across_f = down.astype(F32), across.astype(F32)
    for k in range(2):
        match[:, k * tiles : (k + 1) * tiles] = jnp.where(
            (owner_col == across_f) & (rank_col == k), 1.0, 0.0
        )
    starts = column(start[...]).astype(jnp.int32)
    counts = column(count[...]).astype(jnp.int32)
    shift = starts & (LANES - 1)
    first = starts >> 7
    phase = first & 7
    match[:, 2 * tiles :] = jnp.where(
        across == 0, shift.astype(F32), jnp.where(across == 1, counts.astype(F32), 0.0)
    )
    wide = iota(pattern.shape, 1)
    cells = jnp.where(wide < counts, pattern[...], 0.0)
    for bit in range(7):
        cells = jnp.where((shift >> bit) & 1 == 1, pltpu.roll(cells, 1 << bit, 1), cells)
    front, back = cells[:, :LANES], cells[:, LANES:]
    head = jnp.where(across >= shift, front, 0.0)
    tail = jnp.where(across >= shift, 0.0, front)

    def pick(a, b, c):
        return jnp.where(
            phase == a, head, jnp.where(phase == b, back, jnp.where(phase == c, tail, 0.0))
        )

    low_y = pick(0, 7, 6)
    high_y = pick(7, 6, 5)
    low_corner = pltpu.roll(jnp.where((first + 7) >> 3 == NX - 1, low_y, 0.0), 32, 1)
    high_corner = pltpu.roll(jnp.where(first >> 3 == 0, high_y, 0.0), 96, 1)
    edges = jnp.where(
        across < 32,
        low_y,
        jnp.where(across < 64, low_corner, jnp.where(across < 96, high_corner, high_y)),
    )
    origin = jnp.broadcast_to(starts.astype(F32), square)
    everything = jnp.concatenate([front, back, edges, origin], axis=1)
    choose = [jnp.where((owner_row == down_f) & (rank_row == k), 1.0, 0.0) for k in range(2)]
    every_slot = select_rows(jnp.concatenate(choose, axis=0), everything)
    for k in range(2):
        slots = every_slot[k * tiles : (k + 1) * tiles]
        pair = slots[:, : 2 * LANES]
        edge = slots[:, 2 * LANES : 3 * LANES]
        origins = slots[:, 3 * LANES :]

        def other(values, distance):
            return pltpu.roll(values, -distance % tiles, 0)

        beyond = jnp.where(iota(pair.shape, 0) & 8 == 0, other(pair, -8), other(pair, 8))
        for place, rows in ((0, pair), (6, beyond)):
            for half in range(2):
                message[pl.ds(place + 2 * k + half, tiles, stride=ROWS), :] = rows[
                    :, half * LANES : (half + 1) * LANES
                ]
        corner = jnp.where(down & 8 == 0, other(edge, -7), pltpu.roll(other(edge, 7), 96, 1))
        row = jnp.where(across < 32, other(edge, 1), jnp.where(across < 64, corner, other(edge, -1)))
        outer_origins = jnp.where(down & 8 == 0, other(origins, -8), other(origins, 8))
        for place, moved in enumerate((origins, other(origins, 1), other(origins, -1), outer_origins)):
            row = jnp.where(across == META + place, moved, row)
        message[pl.ds(4 + k, tiles, stride=ROWS), :] = row


def prepare_all(
    ef, hf, ea, ha, perm, pattern_hbm, owner_hbm, count_hbm, start_hbm,
    inner_y, outer_y, message, match,
    first, last, first_perm, last_perm,
    pattern, owner, count, start, sems,
):
    small = [(owner_hbm, owner), (count_hbm, count), (start_hbm, start), (pattern_hbm, pattern)]
    loads_y = []
    for dest, dest_perm, low in ((first, first_perm, 0), (last, last_perm, NY - 8)):
        rows = pl.ds(low, 8)
        for i, src in enumerate((ef, ea, hf, ha)):
            loads_y.append((src.at[:, :, rows], dest.at[pl.ds(3 * i, 3)]))
        loads_y.append((perm.at[:, rows], dest_perm))
    copies = [
        pltpu.make_async_copy(a, b, sems.at[i]) for i, (a, b) in enumerate(small + loads_y)
    ]
    for copy in copies:
        copy.start()
    for copy in copies[:4]:
        copy.wait()
    pack_tiles(pattern, owner, count, start, message, match)
    for copy in copies[4:]:
        copy.wait()

    def fill(up, down):
        for to_next, src, src_perm, out in ((True, last, last_perm, up), (False, first, first_perm, down)):
            flat = src.reshape(12 * NX * 8, LANES)
            flat_perm = src_perm.reshape(NX * 8, LANES)
            at = 0
            for evolution in range(2):
                for field, comp, begin, planes in plan_y(to_next):
                    for k in range(planes):
                        row = (field * 6 + evolution * 3 + comp) * NX * 8 + (begin + k) % 8
                        out[pl.ds(at * NX, NX), :] = flat[pl.ds(row, NX, stride=8), :]
                        at += 1
            out[pl.ds(at * NX, NX), :] = flat_perm[pl.ds(7 if to_next else 0, NX, stride=8), :]
        down[DOWN_ROWS * NX :] = jnp.zeros(((UP_ROWS - DOWN_ROWS) * NX, LANES), F32)

    to_pairs("gy", fill, inner_y, outer_y)


def prepare(ef, hf, ea, ha, perm, pattern, owners, tile_count, tile_start):
    tiles = pattern.shape[0]
    return pl.pallas_call(
        prepare_all,
        out_shape=(
            shape(UP_ROWS * NX, LANES),
            shape(UP_ROWS * NX, LANES),
            shape(tiles * ROWS, LANES),
            shape(tiles, 3 * tiles),
        ),
        in_specs=[hbm()] * 9,
        out_specs=(vmem(),) * 4,
        scratch_shapes=[
            pltpu.VMEM((12, NX, 8, LANES), F32),
            pltpu.VMEM((12, NX, 8, LANES), F32),
            pltpu.VMEM((NX, 8, LANES), F32),
            pltpu.VMEM((NX, 8, LANES), F32),
            pltpu.VMEM((tiles, 2 * LANES), F32),
            pltpu.VMEM((1, tiles), jnp.int32),
            pltpu.VMEM((1, tiles), jnp.int32),
            pltpu.VMEM((1, tiles), jnp.int32),
            pltpu.SemaphoreType.DMA((14,)),
        ],
        compiler_params=params(56),
        cost_estimate=cost(3),
        name="prepare",
    )(
        ef, hf, ea, ha, perm, pattern,
        owners.reshape(1, tiles), tile_count.reshape(1, tiles), tile_start.reshape(1, tiles),
    )


def to_pairs(axis, fill, inner, outer):
    even = lax.axis_index(axis) % 2 == 0
    pl.when(even)(lambda: fill(inner, outer))
    pl.when(jnp.logical_not(even))(lambda: fill(outer, inner))


def from_pairs(axis, inner, outer):
    even = lax.axis_index(axis) % 2 == 0

    def rows(from_prev, begin, count):
        near, far = (outer, inner) if from_prev else (inner, outer)
        return jnp.where(even, near[pl.ds(begin, count), :], far[pl.ds(begin, count), :])

    return rows


def after_y(values):
    return pltpu.roll(values, values.shape[0] - 1, 0)


def before_y(values):
    return pltpu.roll(values, 1, 0)


def after_z(values):
    return jnp.where(iota(values.shape, 1) == LANES - 1, 0.0, pltpu.roll(values, LANES - 1, 1))


def before_z(values):
    return jnp.where(iota(values.shape, 1) == 0, 0.0, pltpu.roll(values, 1, 1))


def curl_e(here, ahead):
    ex, ey, ez = here
    next_y, next_z = ahead
    return (
        (after_y(ez) - ez) - (after_z(ey) - ey),
        (after_z(ex) - ex) - (next_z - ez),
        (next_y - ey) - (after_y(ex) - ex),
    )


def curl_h(here, behind):
    hx, hy, hz = here
    last_y, last_z = behind
    return (
        (hz - before_y(hz)) - (hy - before_z(hy)),
        (hx - before_z(hx)) - (hz - last_z),
        (hy - last_y) - (hx - before_y(hx)),
    )


def start_row(meta_rows, k, index):
    return meta_rows[k][META + index : META + index + 1, :].astype(jnp.int32)


def start_col(meta, k, index):
    return meta[k][:, META + index : META + index + 1].astype(jnp.int32)


def step_one(
    ef, hf, ea, ha, perm, inner_any, outer_any, inner_y_any, outer_y_any, message_any,
    final, overlap, sigma_out, state, inner_out,
    forward, adjoint, perm_wide, grow, e_out, h_out, turned, rate, final_v, outer_local,
    inner, outer, inner_y, outer_y, message, sems,
):
    wide = (forward, adjoint)
    loads = [(src, wide[i // 2].at[pl.ds(3 * (i % 2), 3), :, pl.ds(0, NY)]) for i, src in enumerate((ef, hf, ea, ha))]
    pairs = [(message_any, message), (inner_y_any, inner_y), (outer_y_any, outer_y)]
    pairs += [(perm, perm_wide.at[:, pl.ds(0, NY)]), (inner_any, inner), (outer_any, outer)]
    pairs += loads
    copies = [pltpu.make_async_copy(a, b, sems.at[i]) for i, (a, b) in enumerate(pairs)]
    for copy in copies:
        copy.start()
    copies[0].wait()
    tiles = message.shape[0] // ROWS
    square = (tiles, LANES)
    across = iota(square, 1)
    block = NX * 8

    def rows_of(place):
        return message[pl.ds(place, tiles, stride=ROWS), :]

    meta = [rows_of(4), rows_of(5)]
    meta_rows = [rows.T for rows in meta]
    even = lax.axis_index("gx") % 2 == 0

    def place_cells(place, index, row):
        targets, values = [], []
        for k in range(2):
            first = start_row(meta_rows, k, index) >> 7
            shift = start_col(meta, k, index) & (LANES - 1)
            front, back = rows_of(place + 2 * k), rows_of(place + 2 * k + 1)
            head, tail = jnp.where(across >= shift, front, 0.0), jnp.where(across >= shift, 0.0, front)
            for step, part in enumerate((head, back, tail)):
                targets.append(jnp.where(first + step == row, 1.0, 0.0))
                values.append(part)
        return select_rows(jnp.concatenate(targets, axis=1), jnp.concatenate(values, axis=0))

    density = place_cells(0, 0, iota((block, tiles), 0))
    beyond = place_cells(6, 3, iota((16, tiles), 0) + jnp.where(even, block - 8, 0))[:8]
    sigma = jax.nn.sigmoid(density)
    sigma_out[...] = sigma
    own = CONTRAST * sigma
    targets = []
    row = iota((3 * NX, tiles), 0)
    for k in range(2):
        first = start_row(meta_rows, k, 1) >> 7
        last = start_row(meta_rows, k, 2) >> 7
        targets.append(
            jnp.where(
                (((first + 7) >> 3 == row) & (row < NX))
                | ((last >> 3) + NX == row)
                | (row >= 2 * NX),
                1.0,
                0.0,
            )
        )
    sides = CONTRAST * jax.nn.sigmoid(
        select_rows(jnp.concatenate(targets, axis=1), jnp.concatenate(meta, axis=0))
    )

    def lanes_to(values, source):
        lane = iota(values.shape, 1)
        moved = pltpu.roll(values, (LOWER - source) % LANES, 1)
        return jnp.where((lane >= LOWER) & (lane < LOWER + LAYERS), moved, 0.0)

    for quarter in range(4):
        moved = lanes_to(own, quarter * LAYERS)
        for x in range(NX):
            grow[pl.ds(x * EY + quarter, 8, stride=4), :] = moved[8 * x : 8 * x + 8]
    grow[pl.ds(NY, NX, stride=EY), :] = lanes_to(sides[:NX], 0)
    grow[pl.ds(EY - 1, NX, stride=EY), :] = lanes_to(sides[NX : 2 * NX], 96)
    beyond = CONTRAST * jax.nn.sigmoid(beyond)
    for quarter in range(4):
        grow[pl.ds(NX * EY + quarter, 8, stride=4), :] = lanes_to(beyond, quarter * LAYERS)
    corner = sides[2 * NX : 2 * NX + 8]
    grow[pl.ds(NX * EY + NY, 1), :] = lanes_to(corner, 32)[:1]
    grow[pl.ds(NX * EY + EY - 1, 1), :] = lanes_to(corner, 32)[:1]

    low_x = lax.axis_index("gx") > 0
    gy = lax.axis_index("gy")
    low_y, high_y = gy > 0, gy < lax.axis_size("gy") - 1
    y = iota((EY, LANES), 0)
    within = (y < NY) | ((y == NY) & high_y) | ((y == EY - 1) & low_y)
    cut = jnp.where((y < EY - 2) | low_y, COURANT, 0.0)
    edge_cut = jnp.where(low_x, cut, 0.0)
    nothing = jnp.zeros((EY, LANES), F32)
    for copy in copies[1:6]:
        copy.wait()
    flat_perm = perm_wide.reshape(NX * EY, LANES)
    beside_y = from_pairs("gy", inner_y, outer_y)
    flat_perm[pl.ds(EY - 1, NX, stride=EY), :] = beside_y(True, (UP_ROWS - 1) * NX, NX)
    flat_perm[pl.ds(NY, NX, stride=EY), :] = beside_y(False, (DOWN_ROWS - 1) * NX, NX)

    def halo_plane(src, planes, at):
        begin, row = planes * NY + 3 * at, iota((8, LANES), 0)
        tile = nothing[:8]
        for k in range(3):
            tile = jnp.where(row == BESIDE[k] - NY, src[begin + k : begin + k + 1], tile)
        return jnp.concatenate([src[at * NY : (at + 1) * NY], tile], axis=0)

    def e_ahead(evolution, c):
        return jnp.where(
            even,
            halo_plane(inner, PLANES, 2 * evolution + c - 1),
            halo_plane(outer, DOWN_X, 5 * evolution + c - 1),
        )

    def h_behind(evolution, c):
        return jnp.where(
            even,
            halo_plane(outer, UP_X, 8 * evolution + 3 + c),
            halo_plane(inner, PLANES, 2 * evolution + c - 1),
        )

    for evolution in range(2):
        e, fields = 3 * evolution, wide[evolution]
        for copy in copies[6 + 2 * evolution : 8 + 2 * evolution]:
            copy.wait()
        flat = fields.reshape(6 * NX * EY, LANES)
        for from_prev, planes in ((True, UP_ROWS), (False, DOWN_ROWS)):
            at = evolution * (planes // 2)
            for field, comp, begin, count in plan_y(from_prev):
                for k in range(count):
                    row = EY + begin + k if from_prev else NY + begin + k
                    place = (field * 3 + comp) * NX * EY + row
                    flat[pl.ds(place, NX, stride=EY), :] = beside_y(from_prev, at * NX, NX)
                    at += 1
        for x in range(NX):
            here = [fields[c, x] for c in range(3)]
            if x < NX - 1:
                ahead = [fields[c, x + 1] for c in (1, 2)]
            else:
                ahead = [e_ahead(evolution, c) for c in (1, 2)]
            curl = curl_e(here, ahead)
            for c in range(3):
                h_out[e + c, x] = fields[3 + c, x] - cut * curl[c]
        for x in range(NX):
            if evolution:
                scale = grow[pl.ds(x * EY, EY), :]
            else:
                eps = perm_wide[x] + grow[pl.ds(x * EY, EY), :]
                scale = jnp.where(within, COURANT / eps, 0.0)
                grow[pl.ds(x * EY, EY), :] = scale
                rate[x] = scale[:NY]
            here = [h_out[e + c, x] for c in range(3)]
            if x > 0:
                behind = [h_out[e + c, x - 1] for c in (1, 2)]
            else:
                behind = [
                    h_behind(evolution, 1) + edge_cut * fields[2, 0],
                    h_behind(evolution, 2) - edge_cut * fields[1, 0],
                ]
            curl = curl_h(here, behind)
            for c in range(3):
                e_out[e + c, x] = fields[c, x] + scale * curl[c]

    def outer_rate(planes, inside, rows):
        eps = halo_plane(outer, planes, planes - 1) + grow[pl.ds(NX * EY, EY), :]
        return jnp.where(rows & inside, COURANT / eps, 0.0)

    def put_up(out, evolution, h, e, factor):
        curl = curl_e(e, [nothing, nothing])
        for c in (1, 2):
            at = (2 * evolution + c - 1) * NY
            out[at : at + NY] = (h[c] - factor * curl[c])[:NY]

    def put_down(out, evolution, e_y, e_z):
        at = 2 * evolution * NY
        out[at : at + NY] = e_y[:NY]
        out[at + NY : at + 2 * NY] = e_z[:NY]
        at = PLANES * NY + evolution
        out[at : at + 1] = e_y[EY - 1 :]

    for out in (inner_out, outer_local):
        out[PLANES * NY :] = jnp.zeros((8, LANES), F32)

    def even_device():
        scale = outer_rate(UP_X, low_x, within & (y < EY - 1))
        for evolution in range(2):
            e = 3 * evolution
            last = [e_out[e + c, NX - 1] for c in range(3)]
            put_up(inner_out, evolution, [h_out[e + c, NX - 1] for c in range(3)], last, cut)
            electric, magnetic = [
                [halo_plane(outer, UP_X, 8 * evolution + i + c) for c in range(3)] for i in (0, 3)
            ]
            start = wide[evolution]
            magnetic[1] = magnetic[1] + edge_cut * start[2, 0]
            magnetic[2] = magnetic[2] - edge_cut * start[1, 0]
            curl = curl_h(magnetic, [halo_plane(outer, UP_X, 8 * evolution + 6 + c) for c in range(2)])
            electric = [electric[c] + scale * curl[c] for c in range(3)]
            put_up(outer_local, evolution, magnetic, electric, edge_cut)

    def odd_device():
        scale = outer_rate(DOWN_X, lax.axis_index("gx") < lax.axis_size("gx") - 1, within & (y != NY))
        for evolution in range(2):
            e = 3 * evolution
            put_down(inner_out, evolution, e_out[e + 1, 0], e_out[e + 2, 0])
            planes = [halo_plane(outer, DOWN_X, 5 * evolution + i) for i in range(5)]
            curl = curl_h(planes[2:], [h_out[e + c, NX - 1] for c in (1, 2)])
            put_down(outer_local, evolution, planes[0] + scale * curl[1], planes[1] + scale * curl[2])

    pl.when(even)(even_device)
    pl.when(jnp.logical_not(even))(odd_device)

    def ahead_plane(at, evolution):
        tile = jnp.where(iota((8, LANES), 0) == 7, outer_local[pl.ds(PLANES * NY + evolution, 1), :], 0.0)
        plane = jnp.concatenate([outer_local[pl.ds(at * NY, NY), :], tile], axis=0)
        return jnp.where(even, 0.0, plane)

    for x in range(NX):
        for evolution in range(2):
            e = 3 * evolution
            here = [e_out[e + c, x] for c in range(3)]
            if x < NX - 1:
                ahead = [e_out[e + c, x + 1] for c in (1, 2)]
            else:
                ahead = [ahead_plane(2 * evolution + c, evolution) for c in range(2)]
            curl = curl_e(here, ahead)
            for c in range(3):
                turned[e + c, x] = h_out[e + c, x] - cut * curl[c]
    leaving = []
    for evolution in range(2):
        e, at = 3 * evolution, 2 * evolution * NY
        for x in range(NX):
            if x > 0:
                behind = [turned[e + c, x - 1][:NY] for c in (1, 2)]
            else:
                factor = edge_cut[:NY]
                behind = [
                    outer_local[pl.ds(at, NY), :] + factor * e_out[e + 2, 0][:NY],
                    outer_local[pl.ds(at + NY, NY), :] - factor * e_out[e + 1, 0][:NY],
                ]
            old = [e_out[e + c, x][:NY] for c in range(3)]
            new = last_e(old, rate[x], [turned[e + c, x] for c in range(3)], behind)
            if evolution:
                forward_old = [e_out[c, x][:NY] for c in range(3)]
                forward_new = [final_v[c, x] for c in range(3)]
                overlap[pl.ds(x * NY, NY), :] = product([forward_old, old], [forward_new, new])
            else:
                for c in range(3):
                    final_v[c, x] = new[c]
                if x % 4 == 3:
                    part = pl.ds(x - 3, 4)
                    leaving.append(
                        pltpu.make_async_copy(final_v.at[:, part], final.at[:, part], sems.at[10 + x // 4])
                    )
                    leaving[-1].start()

    def keep(x):
        for c in range(6):
            state[c] = e_out[c, x]
            state[6 + c] = turned[c, x]
        for evolution in range(2):
            for c in (1, 2):
                state[11 + 2 * evolution + c] = turned[3 * evolution + c, NX - 2]
        state[16, :NY] = rate[x]
        state[16, NY:] = nothing[NY:]

    pl.when(even)(lambda: keep(NX - 1))
    pl.when(jnp.logical_not(even))(lambda: keep(0))
    for copy in leaving:
        copy.wait()


def last_e(electric, scale, magnetic, behind):
    last_x, last_z = before_y(magnetic[0])[:NY], before_y(magnetic[2])[:NY]
    hx, hy, hz = [v[:NY] for v in magnetic]
    curl = (
        (hz - last_z) - (hy - before_z(hy)),
        (hx - before_z(hx)) - (hz - behind[1]),
        (hy - behind[0]) - (hx - last_x),
    )
    return [electric[c] + scale * curl[c] for c in range(3)]


def product(old, new):
    blend = math.cos(ANGULAR)
    total = 0.0
    for c in range(3):
        total += old[0][c] * (old[1][c] + blend * new[1][c])
        total += new[0][c] * (new[1][c] + blend * old[1][c])
    return total


def first_step(ef, hf, ea, ha, perm, inner, outer, inner_y, outer_y, message):
    return pl.pallas_call(
        step_one,
        out_shape=(
            shape(3, NX, NY, LANES),
            shape(NX * NY, LANES),
            shape(NX * 8, LANES),
            shape(17, EY, LANES),
            shape(PLANES * NY + 8, LANES),
        ),
        in_specs=[hbm()] * 5 + [anywhere()] * 5,
        out_specs=(hbm(),) + (vmem(),) * 4,
        scratch_shapes=[
            pltpu.VMEM((6, NX, EY, LANES), F32),
            pltpu.VMEM((6, NX, EY, LANES), F32),
            pltpu.VMEM((NX, EY, LANES), F32),
            pltpu.VMEM(((NX + 1) * EY, LANES), F32),
            pltpu.VMEM((6, NX, EY, LANES), F32),
            pltpu.VMEM((6, NX, EY, LANES), F32),
            pltpu.VMEM((6, NX, EY, LANES), F32),
            pltpu.VMEM((NX, NY, LANES), F32),
            pltpu.VMEM((3, NX, NY, LANES), F32),
            pltpu.VMEM((PLANES * NY + 8, LANES), F32),
            pltpu.VMEM(inner.shape, F32),
            pltpu.VMEM(outer.shape, F32),
            pltpu.VMEM(inner_y.shape, F32),
            pltpu.VMEM(outer_y.shape, F32),
            pltpu.VMEM(message.shape, F32),
            pltpu.SemaphoreType.DMA((14,)),
        ],
        compiler_params=params(51),
        cost_estimate=cost(5),
        name="step_one",
    )(ef, hf, ea, ha, perm, inner, outer, inner_y, outer_y, message)


def step_two(final_in, overlap_in, sigma_in, state, inner, message, final, reply, plane, overlap, sem):
    even = lax.axis_index("gx") % 2 == 0
    low_y = lax.axis_index("gy") > 0
    y = iota((EY, LANES), 0)
    cut = jnp.where(((y < EY - 2) | low_y) & even, COURANT, 0.0)
    x = jnp.where(even, NX - 1, 0)
    overlap[...] = overlap_in[...]
    old, new = [], []
    for evolution in range(2):
        e, at = 3 * evolution, 2 * evolution * NY
        rows = [inner[at + c * NY : at + (c + 1) * NY] for c in range(2)]
        beside = inner[PLANES * NY + evolution : PLANES * NY + evolution + 1]
        tile = jnp.where(iota((8, LANES), 0) == 7, beside, 0.0)
        ahead = [jnp.concatenate([r, tile], axis=0) for r in rows]
        old.append([state[e + c][:NY] for c in range(3)])
        magnetic = [state[6 + e], state[7 + e] + cut * ahead[1], state[8 + e] - cut * ahead[0]]
        behind = [
            jnp.where(even, state[12 + 2 * evolution][:NY], rows[0] + COURANT * old[-1][2]),
            jnp.where(even, state[13 + 2 * evolution][:NY], rows[1] - COURANT * old[-1][1]),
        ]
        new.append(last_e(old[-1], state[16][:NY], magnetic, behind))
    for c in range(3):
        plane[c] = new[0][c]
    final_copy = pltpu.make_async_copy(plane, final.at[:, x], sem)
    final_copy.start()
    overlap[pl.ds(pl.multiple_of(x * NY, NY), NY), :] = product(old, new)
    tiles = message.shape[0] // ROWS
    across = iota((tiles, LANES), 1)
    meta = [message[pl.ds(4 + k, tiles, stride=ROWS), :] for k in range(2)]
    block = NX * 8
    compact = jnp.zeros((block, LANES), F32)
    lane = iota((block, LANES), 1)
    for quarter in range(4):
        part = pltpu.roll(
            overlap[pl.ds(quarter, block, stride=4), :], (quarter * LAYERS - LOWER) % LANES, 1
        )
        compact = jnp.where(lane // LAYERS == quarter, part, compact)
    sigma = sigma_in[...]
    gradient = CONTRAST * sigma * (1.0 - sigma) * compact
    picks, shifts = [], []
    for k in range(2):
        starts = start_col(meta, k, 0)
        shifts.append(starts & (LANES - 1))
        for step in range(3):
            picks.append(jnp.where(iota((tiles, block), 1) == (starts >> 7) + step, 1.0, 0.0))
    found = select_rows(jnp.concatenate(picks, axis=0), gradient)
    for k in range(2):
        head, back, tail = [found[(3 * k + i) * tiles : (3 * k + i + 1) * tiles] for i in range(3)]
        reply[pl.ds(2 * k, tiles, stride=4), :] = jnp.where(across >= shifts[k], head, tail)
        reply[pl.ds(2 * k + 1, tiles, stride=4), :] = back
    final_copy.wait()


def second_step(final, overlap, sigma, state, inner, message):
    tiles = message.shape[0] // ROWS
    return pl.pallas_call(
        step_two,
        out_shape=(shape(3, NX, NY, LANES), shape(tiles * 4, LANES)),
        in_specs=[hbm()] + [vmem()] * 5,
        out_specs=(hbm(), vmem()),
        input_output_aliases={0: 0},
        scratch_shapes=[
            pltpu.VMEM((3, NY, LANES), F32),
            pltpu.VMEM((NX * NY, LANES), F32),
            pltpu.SemaphoreType.DMA,
        ],
        compiler_params=params(30),
        cost_estimate=cost(1),
        name="step_two",
    )(final, overlap, sigma, state, inner, message)


def unpack_tiles(reply, match, out):
    tiles = out.shape[0]
    shift = match[:, 2 * tiles : 2 * tiles + 1].astype(jnp.int32)
    count = match[:, 2 * tiles + 1 : 2 * tiles + 2].astype(jnp.int32)
    rows = [
        jnp.concatenate(
            [reply[pl.ds(2 * k + half, tiles, stride=4), :] for half in range(2)], axis=1
        )
        for k in range(2)
    ]
    cells = select_rows(match[:, : 2 * tiles], jnp.concatenate(rows, axis=0))
    width = out.shape[1]
    for bit in range(7):
        cells = jnp.where((shift >> bit) & 1 == 1, pltpu.roll(cells, width - (1 << bit), 1), cells)
    out[...] = jnp.where(iota(out.shape, 1) < count, cells, 0.0)


def unpack(reply, match):
    tiles = match.shape[0]
    return pl.pallas_call(
        unpack_tiles,
        out_shape=shape(tiles, 2 * LANES),
        in_specs=[vmem()] * 2,
        out_specs=vmem(),
        compiler_params=params(16),
        cost_estimate=cost(2),
        name="unpack_tiles",
    )(reply, match)


def swapped(block, axis, first):
    pairs = [(i, i + 1) for i in range(first, lax.axis_size(axis) - 1, 2)]
    return lax.ppermute(block, axis, pairs + [(j, i) for i, j in pairs])


def exchange(block, depth):
    out = lax.all_to_all(
        block.reshape(-1, depth, LANES), ("gx", "gy"), split_axis=0, concat_axis=0, tiled=True
    )
    return out.reshape(block.shape)


def faces_x(ef, hf, ea, ha, perm, inner_y, outer_y, inner_out, outer_out, first_x, last_x, edge_perm, tiles, sems):
    pairs = []
    for i, src in enumerate((ef, ea, hf, ha)):
        pairs.append((src.at[:, pl.ds(NX - 2, 2)], last_x.at[pl.ds(3 * i, 3)]))
        pairs.append((src.at[:, pl.ds(0, 2)], first_x.at[pl.ds(3 * i, 3)]))
    pairs.append((perm.at[NX - 1], edge_perm.at[0]))
    pairs.append((perm.at[0], edge_perm.at[1]))
    copies = [pltpu.make_async_copy(a, b, sems.at[i]) for i, (a, b) in enumerate(pairs)]
    for copy in copies:
        copy.start()
    beside = from_pairs("gy", inner_y, outer_y)
    for from_prev in (True, False):
        at = 0
        for evolution in range(2):
            for field, comp, begin, count in plan_y(from_prev):
                for k in range(count):
                    row = 8 + begin + k if from_prev else begin + k
                    for i, x in enumerate((NX - 2, NX - 1, 0, 1)):
                        tiles[field * 6 + evolution * 3 + comp, i, row : row + 1, :] = beside(
                            from_prev, at * NX + x, 1
                        )
                    at += 1
    for copy in copies:
        copy.wait()

    def plane(c, i):
        block = last_x[c, i] if i < 2 else first_x[c, i - 2]
        return jnp.concatenate([block, tiles[c, i]], axis=0)

    def send(out, planes, at, values):
        out[at * NY : (at + 1) * NY] = values[:NY]
        for k, row in enumerate(BESIDE):
            out[planes * NY + 3 * at + k : planes * NY + 3 * at + k + 1] = values[row : row + 1]

    def send_perm(out, planes, i, x):
        at = planes - 1
        out[at * NY : (at + 1) * NY] = edge_perm[i]
        for k, (from_prev, count) in enumerate(((True, UP_ROWS), (False, DOWN_ROWS))):
            begin = planes * NY + 3 * at + k
            out[begin : begin + 1] = beside(from_prev, (count - 1) * NX + x, 1)
        out[planes * TALL - 1 :] = jnp.zeros((outer_out.shape[0] - planes * TALL + 1, LANES), F32)

    inside_y = lax.axis_index("gy") > 0
    rate = jnp.where((iota((EY, LANES), 0) < EY - 2) | inside_y, COURANT, 0.0)
    nothing = jnp.zeros((EY, LANES), F32)

    def even_device():
        for evolution in range(2):
            e, h = 3 * evolution, 6 + 3 * evolution
            curl = curl_e([plane(e + c, 1) for c in range(3)], [nothing, nothing])
            for c in (1, 2):
                send(inner_out, PLANES, 2 * evolution + c - 1, plane(h + c, 1) - rate * curl[c])
            first, second = [[plane(e + c, i) for c in range(3)] for i in (2, 3)]
            curl = curl_e(first, second[1:])
            planes = first[1:] + [plane(h + c, 2) - rate * curl[c] for c in range(3)]
            for i, values in enumerate(planes):
                send(outer_out, DOWN_X, 5 * evolution + i, values)
        send_perm(outer_out, DOWN_X, 1, 0)

    def odd_device():
        for evolution in range(2):
            e, h = 3 * evolution, 6 + 3 * evolution
            for c in (1, 2):
                send(inner_out, PLANES, 2 * evolution + c - 1, plane(e + c, 2))
            before_last, last = [[plane(e + c, i) for c in range(3)] for i in (0, 1)]
            curl = curl_e(before_last, last[1:])
            planes = [plane(h + c, 0) - rate * curl[c] for c in (1, 2)]
            curl = curl_e(last, [nothing, nothing])
            planes = last + [plane(h + c, 1) - rate * curl[c] for c in range(3)] + planes
            for i, values in enumerate(planes):
                send(outer_out, UP_X, 8 * evolution + i, values)
        send_perm(outer_out, UP_X, 0, NX - 1)

    even = lax.axis_index("gx") % 2 == 0
    pl.when(even)(even_device)
    pl.when(jnp.logical_not(even))(odd_device)


def send_x(ef, hf, ea, ha, perm, inner_y, outer_y):
    return pl.pallas_call(
        faces_x,
        out_shape=(shape(PLANES * TALL, LANES), shape(UP_X * TALL, LANES)),
        in_specs=[hbm()] * 5 + [vmem()] * 2,
        out_specs=(vmem(), vmem()),
        scratch_shapes=[
            pltpu.VMEM((12, 2, NY, LANES), F32),
            pltpu.VMEM((12, 2, NY, LANES), F32),
            pltpu.VMEM((2, NY, LANES), F32),
            pltpu.VMEM((12, 4, 8, LANES), F32),
            pltpu.SemaphoreType.DMA((10,)),
        ],
        compiler_params=params(50),
        cost_estimate=cost(20),
        name="faces_x",
    )(ef, hf, ea, ha, perm, inner_y, outer_y)


def shards(ef, hf, ea, ha, perm, pattern, owners, tile_count, tile_start):
    inner_y, outer_y, message, match = prepare(
        ef, hf, ea, ha, perm, pattern, owners, tile_count, tile_start
    )
    outer_y, inner_y = swapped(outer_y, "gy", 1), swapped(inner_y, "gy", 0)
    arrived = exchange(message, 1)
    inner, outer = send_x(ef, hf, ea, ha, perm, inner_y, outer_y)
    outer, inner = swapped(outer, "gx", 1), swapped(inner, "gx", 0)
    *state, inner = first_step(
        ef, hf, ea, ha, perm, inner, outer, inner_y, outer_y, arrived
    )
    final, reply = second_step(*state, swapped(inner, "gx", 0), arrived)
    return final, unpack(exchange(reply, 4), match)


def solution(mesh):
    grid = P(None, "gx", "gy", None)
    tiles = ("gx", "gy")
    return jax.shard_map(
        shards,
        mesh=mesh,
        in_specs=(grid,) * 4 + (P("gx", "gy", None), P(tiles, None), P(tiles, None), P(tiles), P(tiles)),
        out_specs=(grid, P(tiles, None)),
        check_vma=False,
    )
```

```python
import functools
import math

import jax
import jax.numpy as jnp
from jax import lax
from jax.experimental import pallas as pl
from jax.experimental.pallas import tpu as pltpu
from jax.sharding import PartitionSpec as P

F32 = jnp.float32
LANES = 128
LAYERS = 32
LOWER = 48
COURANT = 0.5
ANGULAR = 0.9
CONTRAST = 8.0
EXACT = lax.Precision.HIGHEST

NX, NY = 16, 32
EY = 40
UP_ROWS = 23
DOWN_ROWS = 17
PLANES = 4
UP_X = 17
DOWN_X = 11
BESIDE = (EY - 1, NY, EY - 2)
TALL = NY + len(BESIDE)
ROWS = 10
META = 64


def iota(shape, dim):
    return lax.broadcasted_iota(jnp.int32, shape, dim)


def params(limit):
    return pltpu.CompilerParams(vmem_limit_bytes=limit * 2**20)


def cost(micros):
    return pl.CostEstimate(flops=micros * 10**9, bytes_accessed=0, transcendentals=0)


def vmem():
    return pl.BlockSpec(memory_space=pltpu.VMEM)


def anywhere():
    return pl.BlockSpec(memory_space=pl.ANY)


def hbm():
    return pl.BlockSpec(memory_space=pltpu.HBM)


def shape(*dims):
    return jax.ShapeDtypeStruct(dims, F32)


def select_rows(marks, values):
    width = values.shape[1]
    high = values.astype(jnp.bfloat16)
    low = (values - high.astype(F32)).astype(jnp.bfloat16)
    found = jnp.dot(
        marks.astype(jnp.bfloat16),
        jnp.concatenate([high, low], axis=1),
        preferred_element_type=F32,
    )
    return found[:, :width] + found[:, width:]


def plan_y(to_next):
    if to_next:
        return [(0, 0, -2, 2), (0, 1, -2, 2), (0, 2, -2, 2), (1, 0, -2, 2), (1, 1, -1, 1), (1, 2, -2, 2)]
    return [(0, 0, 0, 2), (0, 1, 0, 1), (0, 2, 0, 2), (1, 0, 0, 1), (1, 1, 0, 1), (1, 2, 0, 1)]


def pack_tiles(pattern, owner, count, start, message, match):
    tiles = pattern.shape[0]
    square = (tiles, tiles)
    down, across = iota(square, 0), iota(square, 1)
    eye = down == across

    def column(row):
        return jnp.sum(jnp.where(eye, row.astype(F32), 0.0), axis=1, keepdims=True)

    owner_row = owner[...].astype(F32)
    owner_col = column(owner[...])
    same = owner_col == owner_row
    rank_row = jnp.sum(jnp.where(same & (down < across), 1.0, 0.0), axis=0, keepdims=True)
    rank_col = jnp.sum(jnp.where(same & (across < down), 1.0, 0.0), axis=1, keepdims=True)
    down_f, across_f = down.astype(F32), across.astype(F32)
    for k in range(2):
        match[:, k * tiles : (k + 1) * tiles] = jnp.where(
            (owner_col == across_f) & (rank_col == k), 1.0, 0.0
        )
    starts = column(start[...]).astype(jnp.int32)
    counts = column(count[...]).astype(jnp.int32)
    shift = starts & (LANES - 1)
    first = starts >> 7
    phase = first & 7
    match[:, 2 * tiles :] = jnp.where(
        across == 0, shift.astype(F32), jnp.where(across == 1, counts.astype(F32), 0.0)
    )
    wide = iota(pattern.shape, 1)
    cells = jnp.where(wide < counts, pattern[...], 0.0)
    for bit in range(7):
        cells = jnp.where((shift >> bit) & 1 == 1, pltpu.roll(cells, 1 << bit, 1), cells)
    front, back = cells[:, :LANES], cells[:, LANES:]
    head = jnp.where(across >= shift, front, 0.0)
    tail = jnp.where(across >= shift, 0.0, front)

    def pick(a, b, c):
        return jnp.where(
            phase == a, head, jnp.where(phase == b, back, jnp.where(phase == c, tail, 0.0))
        )

    low_y = pick(0, 7, 6)
    high_y = pick(7, 6, 5)
    low_corner = pltpu.roll(jnp.where((first + 7) >> 3 == NX - 1, low_y, 0.0), 32, 1)
    high_corner = pltpu.roll(jnp.where(first >> 3 == 0, high_y, 0.0), 96, 1)
    edges = jnp.where(
        across < 32,
        low_y,
        jnp.where(across < 64, low_corner, jnp.where(across < 96, high_corner, high_y)),
    )
    origin = jnp.broadcast_to(starts.astype(F32), square)
    everything = jnp.concatenate([front, back, edges, origin], axis=1)
    choose = [jnp.where((owner_row == down_f) & (rank_row == k), 1.0, 0.0) for k in range(2)]
    every_slot = select_rows(jnp.concatenate(choose, axis=0), everything)
    for k in range(2):
        slots = every_slot[k * tiles : (k + 1) * tiles]
        pair = slots[:, : 2 * LANES]
        edge = slots[:, 2 * LANES : 3 * LANES]
        origins = slots[:, 3 * LANES :]

        def other(values, distance):
            return pltpu.roll(values, -distance % tiles, 0)

        beyond = jnp.where(iota(pair.shape, 0) & 8 == 0, other(pair, -8), other(pair, 8))
        for place, rows in ((0, pair), (6, beyond)):
            for half in range(2):
                message[pl.ds(place + 2 * k + half, tiles, stride=ROWS), :] = rows[
                    :, half * LANES : (half + 1) * LANES
                ]
        corner = jnp.where(down & 8 == 0, other(edge, -7), pltpu.roll(other(edge, 7), 96, 1))
        row = jnp.where(across < 32, other(edge, 1), jnp.where(across < 64, corner, other(edge, -1)))
        outer_origins = jnp.where(down & 8 == 0, other(origins, -8), other(origins, 8))
        for place, moved in enumerate((origins, other(origins, 1), other(origins, -1), outer_origins)):
            row = jnp.where(across == META + place, moved, row)
        message[pl.ds(4 + k, tiles, stride=ROWS), :] = row


def prepare_all(
    ef, hf, ea, ha, perm, pattern_hbm, owner_hbm, count_hbm, start_hbm,
    inner_y, outer_y, message, match,
    first, last, first_perm, last_perm,
    pattern, owner, count, start, sems,
):
    small = [(owner_hbm, owner), (count_hbm, count), (start_hbm, start), (pattern_hbm, pattern)]
    loads_y = []
    for dest, dest_perm, low in ((first, first_perm, 0), (last, last_perm, NY - 8)):
        rows = pl.ds(low, 8)
        for i, src in enumerate((ef, ea, hf, ha)):
            loads_y.append((src.at[:, :, rows], dest.at[pl.ds(3 * i, 3)]))
        loads_y.append((perm.at[:, rows], dest_perm))
    copies = [
        pltpu.make_async_copy(a, b, sems.at[i]) for i, (a, b) in enumerate(small + loads_y)
    ]
    for copy in copies:
        copy.start()
    for copy in copies[:4]:
        copy.wait()
    pack_tiles(pattern, owner, count, start, message, match)
    for copy in copies[4:]:
        copy.wait()

    def fill(up, down):
        for to_next, src, src_perm, out in ((True, last, last_perm, up), (False, first, first_perm, down)):
            flat = src.reshape(12 * NX * 8, LANES)
            flat_perm = src_perm.reshape(NX * 8, LANES)
            at = 0
            for evolution in range(2):
                for field, comp, begin, planes in plan_y(to_next):
                    for k in range(planes):
                        row = (field * 6 + evolution * 3 + comp) * NX * 8 + (begin + k) % 8
                        out[pl.ds(at * NX, NX), :] = flat[pl.ds(row, NX, stride=8), :]
                        at += 1
            out[pl.ds(at * NX, NX), :] = flat_perm[pl.ds(7 if to_next else 0, NX, stride=8), :]
        down[DOWN_ROWS * NX :] = jnp.zeros(((UP_ROWS - DOWN_ROWS) * NX, LANES), F32)

    to_pairs("gy", fill, inner_y, outer_y)


def prepare(ef, hf, ea, ha, perm, pattern, owners, tile_count, tile_start):
    tiles = pattern.shape[0]
    return pl.pallas_call(
        prepare_all,
        out_shape=(
            shape(UP_ROWS * NX, LANES),
            shape(UP_ROWS * NX, LANES),
            shape(tiles * ROWS, LANES),
            shape(tiles, 3 * tiles),
        ),
        in_specs=[hbm()] * 9,
        out_specs=(vmem(),) * 4,
        scratch_shapes=[
            pltpu.VMEM((12, NX, 8, LANES), F32),
            pltpu.VMEM((12, NX, 8, LANES), F32),
            pltpu.VMEM((NX, 8, LANES), F32),
            pltpu.VMEM((NX, 8, LANES), F32),
            pltpu.VMEM((tiles, 2 * LANES), F32),
            pltpu.VMEM((1, tiles), jnp.int32),
            pltpu.VMEM((1, tiles), jnp.int32),
            pltpu.VMEM((1, tiles), jnp.int32),
            pltpu.SemaphoreType.DMA((14,)),
        ],
        compiler_params=params(56),
        cost_estimate=cost(3),
        name="prepare",
    )(
        ef, hf, ea, ha, perm, pattern,
        owners.reshape(1, tiles), tile_count.reshape(1, tiles), tile_start.reshape(1, tiles),
    )


def to_pairs(axis, fill, inner, outer):
    even = lax.axis_index(axis) % 2 == 0
    pl.when(even)(lambda: fill(inner, outer))
    pl.when(jnp.logical_not(even))(lambda: fill(outer, inner))


def from_pairs(axis, inner, outer):
    even = lax.axis_index(axis) % 2 == 0

    def rows(from_prev, begin, count):
        near, far = (outer, inner) if from_prev else (inner, outer)
        return jnp.where(even, near[pl.ds(begin, count), :], far[pl.ds(begin, count), :])

    return rows


def after_y(values):
    return pltpu.roll(values, values.shape[0] - 1, 0)


def before_y(values):
    return pltpu.roll(values, 1, 0)


def after_z(values):
    return jnp.where(iota(values.shape, 1) == LANES - 1, 0.0, pltpu.roll(values, LANES - 1, 1))


def before_z(values):
    return jnp.where(iota(values.shape, 1) == 0, 0.0, pltpu.roll(values, 1, 1))


def curl_e(here, ahead):
    ex, ey, ez = here
    next_y, next_z = ahead
    return (
        (after_y(ez) - ez) - (after_z(ey) - ey),
        (after_z(ex) - ex) - (next_z - ez),
        (next_y - ey) - (after_y(ex) - ex),
    )


def curl_h(here, behind):
    hx, hy, hz = here
    last_y, last_z = behind
    return (
        (hz - before_y(hz)) - (hy - before_z(hy)),
        (hx - before_z(hx)) - (hz - last_z),
        (hy - last_y) - (hx - before_y(hx)),
    )


def start_row(meta_rows, k, index):
    return meta_rows[k][META + index : META + index + 1, :].astype(jnp.int32)


def start_col(meta, k, index):
    return meta[k][:, META + index : META + index + 1].astype(jnp.int32)


def step_one(
    ef, hf, ea, ha, perm, inner_any, outer_any, inner_y_any, outer_y_any, message_any,
    final, overlap, sigma_out, state, inner_out,
    forward, adjoint, perm_wide, grow, e_out, h_out, turned, rate, final_v, outer_local,
    inner, outer, inner_y, outer_y, message, sems,
):
    wide = (forward, adjoint)
    loads = [(src, wide[i // 2].at[pl.ds(3 * (i % 2), 3), :, pl.ds(0, NY)]) for i, src in enumerate((ef, hf, ea, ha))]
    pairs = [(message_any, message), (inner_y_any, inner_y), (outer_y_any, outer_y)]
    pairs += [(perm, perm_wide.at[:, pl.ds(0, NY)]), (inner_any, inner), (outer_any, outer)]
    pairs += loads
    copies = [pltpu.make_async_copy(a, b, sems.at[i]) for i, (a, b) in enumerate(pairs)]
    for copy in copies:
        copy.start()
    copies[0].wait()
    tiles = message.shape[0] // ROWS
    square = (tiles, LANES)
    across = iota(square, 1)
    block = NX * 8

    def rows_of(place):
        return message[pl.ds(place, tiles, stride=ROWS), :]

    meta = [rows_of(4), rows_of(5)]
    meta_rows = [rows.T for rows in meta]
    even = lax.axis_index("gx") % 2 == 0

    def place_cells(place, index, row):
        targets, values = [], []
        for k in range(2):
            first = start_row(meta_rows, k, index) >> 7
            shift = start_col(meta, k, index) & (LANES - 1)
            front, back = rows_of(place + 2 * k), rows_of(place + 2 * k + 1)
            head, tail = jnp.where(across >= shift, front, 0.0), jnp.where(across >= shift, 0.0, front)
            for step, part in enumerate((head, back, tail)):
                targets.append(jnp.where(first + step == row, 1.0, 0.0))
                values.append(part)
        return select_rows(jnp.concatenate(targets, axis=1), jnp.concatenate(values, axis=0))

    density = place_cells(0, 0, iota((block, tiles), 0))
    beyond = place_cells(6, 3, iota((16, tiles), 0) + jnp.where(even, block - 8, 0))[:8]
    sigma = jax.nn.sigmoid(density)
    sigma_out[...] = sigma
    own = CONTRAST * sigma
    targets = []
    row = iota((3 * NX, tiles), 0)
    for k in range(2):
        first = start_row(meta_rows, k, 1) >> 7
        last = start_row(meta_rows, k, 2) >> 7
        targets.append(
            jnp.where(
                (((first + 7) >> 3 == row) & (row < NX))
                | ((last >> 3) + NX == row)
                | (row >= 2 * NX),
                1.0,
                0.0,
            )
        )
    sides = CONTRAST * jax.nn.sigmoid(
        select_rows(jnp.concatenate(targets, axis=1), jnp.concatenate(meta, axis=0))
    )

    def lanes_to(values, source):
        lane = iota(values.shape, 1)
        moved = pltpu.roll(values, (LOWER - source) % LANES, 1)
        return jnp.where((lane >= LOWER) & (lane < LOWER + LAYERS), moved, 0.0)

    for quarter in range(4):
        moved = lanes_to(own, quarter * LAYERS)
        for x in range(NX):
            grow[pl.ds(x * EY + quarter, 8, stride=4), :] = moved[8 * x : 8 * x + 8]
    grow[pl.ds(NY, NX, stride=EY), :] = lanes_to(sides[:NX], 0)
    grow[pl.ds(EY - 1, NX, stride=EY), :] = lanes_to(sides[NX : 2 * NX], 96)
    beyond = CONTRAST * jax.nn.sigmoid(beyond)
    for quarter in range(4):
        grow[pl.ds(NX * EY + quarter, 8, stride=4), :] = lanes_to(beyond, quarter * LAYERS)
    corner = sides[2 * NX : 2 * NX + 8]
    grow[pl.ds(NX * EY + NY, 1), :] = lanes_to(corner, 32)[:1]
    grow[pl.ds(NX * EY + EY - 1, 1), :] = lanes_to(corner, 32)[:1]

    low_x = lax.axis_index("gx") > 0
    gy = lax.axis_index("gy")
    low_y, high_y = gy > 0, gy < lax.axis_size("gy") - 1
    y = iota((EY, LANES), 0)
    within = (y < NY) | ((y == NY) & high_y) | ((y == EY - 1) & low_y)
    cut = jnp.where((y < EY - 2) | low_y, COURANT, 0.0)
    edge_cut = jnp.where(low_x, cut, 0.0)
    nothing = jnp.zeros((EY, LANES), F32)
    for copy in copies[1:6]:
        copy.wait()
    flat_perm = perm_wide.reshape(NX * EY, LANES)
    beside_y = from_pairs("gy", inner_y, outer_y)
    flat_perm[pl.ds(EY - 1, NX, stride=EY), :] = beside_y(True, (UP_ROWS - 1) * NX, NX)
    flat_perm[pl.ds(NY, NX, stride=EY), :] = beside_y(False, (DOWN_ROWS - 1) * NX, NX)

    def halo_plane(src, planes, at):
        begin, row = planes * NY + 3 * at, iota((8, LANES), 0)
        tile = nothing[:8]
        for k in range(3):
            tile = jnp.where(row == BESIDE[k] - NY, src[begin + k : begin + k + 1], tile)
        return jnp.concatenate([src[at * NY : (at + 1) * NY], tile], axis=0)

    def e_ahead(evolution, c):
        return jnp.where(
            even,
            halo_plane(inner, PLANES, 2 * evolution + c - 1),
            halo_plane(outer, DOWN_X, 5 * evolution + c - 1),
        )

    def h_behind(evolution, c):
        return jnp.where(
            even,
            halo_plane(outer, UP_X, 8 * evolution + 3 + c),
            halo_plane(inner, PLANES, 2 * evolution + c - 1),
        )

    for evolution in range(2):
        e, fields = 3 * evolution, wide[evolution]
        for copy in copies[6 + 2 * evolution : 8 + 2 * evolution]:
            copy.wait()
        flat = fields.reshape(6 * NX * EY, LANES)
        for from_prev, planes in ((True, UP_ROWS), (False, DOWN_ROWS)):
            at = evolution * (planes // 2)
            for field, comp, begin, count in plan_y(from_prev):
                for k in range(count):
                    row = EY + begin + k if from_prev else NY + begin + k
                    place = (field * 3 + comp) * NX * EY + row
                    flat[pl.ds(place, NX, stride=EY), :] = beside_y(from_prev, at * NX, NX)
                    at += 1
        for x in range(NX):
            here = [fields[c, x] for c in range(3)]
            if x < NX - 1:
                ahead = [fields[c, x + 1] for c in (1, 2)]
            else:
                ahead = [e_ahead(evolution, c) for c in (1, 2)]
            curl = curl_e(here, ahead)
            for c in range(3):
                h_out[e + c, x] = fields[3 + c, x] - cut * curl[c]
        for x in range(NX):
            if evolution:
                scale = grow[pl.ds(x * EY, EY), :]
            else:
                eps = perm_wide[x] + grow[pl.ds(x * EY, EY), :]
                scale = jnp.where(within, COURANT / eps, 0.0)
                grow[pl.ds(x * EY, EY), :] = scale
                rate[x] = scale[:NY]
            here = [h_out[e + c, x] for c in range(3)]
            if x > 0:
                behind = [h_out[e + c, x - 1] for c in (1, 2)]
            else:
                behind = [
                    h_behind(evolution, 1) + edge_cut * fields[2, 0],
                    h_behind(evolution, 2) - edge_cut * fields[1, 0],
                ]
            curl = curl_h(here, behind)
            for c in range(3):
                e_out[e + c, x] = fields[c, x] + scale * curl[c]

    def outer_rate(planes, inside, rows):
        eps = halo_plane(outer, planes, planes - 1) + grow[pl.ds(NX * EY, EY), :]
        return jnp.where(rows & inside, COURANT / eps, 0.0)

    def put_up(out, evolution, h, e, factor):
        curl = curl_e(e, [nothing, nothing])
        for c in (1, 2):
            at = (2 * evolution + c - 1) * NY
            out[at : at + NY] = (h[c] - factor * curl[c])[:NY]

    def put_down(out, evolution, e_y, e_z):
        at = 2 * evolution * NY
        out[at : at + NY] = e_y[:NY]
        out[at + NY : at + 2 * NY] = e_z[:NY]
        at = PLANES * NY + evolution
        out[at : at + 1] = e_y[EY - 1 :]

    for out in (inner_out, outer_local):
        out[PLANES * NY :] = jnp.zeros((8, LANES), F32)

    def even_device():
        scale = outer_rate(UP_X, low_x, within & (y < EY - 1))
        for evolution in range(2):
            e = 3 * evolution
            last = [e_out[e + c, NX - 1] for c in range(3)]
            put_up(inner_out, evolution, [h_out[e + c, NX - 1] for c in range(3)], last, cut)
            electric, magnetic = [
                [halo_plane(outer, UP_X, 8 * evolution + i + c) for c in range(3)] for i in (0, 3)
            ]
            start = wide[evolution]
            magnetic[1] = magnetic[1] + edge_cut * start[2, 0]
            magnetic[2] = magnetic[2] - edge_cut * start[1, 0]
            curl = curl_h(magnetic, [halo_plane(outer, UP_X, 8 * evolution + 6 + c) for c in range(2)])
            electric = [electric[c] + scale * curl[c] for c in range(3)]
            put_up(outer_local, evolution, magnetic, electric, edge_cut)

    def odd_device():
        scale = outer_rate(DOWN_X, lax.axis_index("gx") < lax.axis_size("gx") - 1, within & (y != NY))
        for evolution in range(2):
            e = 3 * evolution
            put_down(inner_out, evolution, e_out[e + 1, 0], e_out[e + 2, 0])
            planes = [halo_plane(outer, DOWN_X, 5 * evolution + i) for i in range(5)]
            curl = curl_h(planes[2:], [h_out[e + c, NX - 1] for c in (1, 2)])
            put_down(outer_local, evolution, planes[0] + scale * curl[1], planes[1] + scale * curl[2])

    pl.when(even)(even_device)
    pl.when(jnp.logical_not(even))(odd_device)

    def ahead_plane(at, evolution):
        tile = jnp.where(iota((8, LANES), 0) == 7, outer_local[pl.ds(PLANES * NY + evolution, 1), :], 0.0)
        plane = jnp.concatenate([outer_local[pl.ds(at * NY, NY), :], tile], axis=0)
        return jnp.where(even, 0.0, plane)

    for x in range(NX):
        for evolution in range(2):
            e = 3 * evolution
            here = [e_out[e + c, x] for c in range(3)]
            if x < NX - 1:
                ahead = [e_out[e + c, x + 1] for c in (1, 2)]
            else:
                ahead = [ahead_plane(2 * evolution + c, evolution) for c in range(2)]
            curl = curl_e(here, ahead)
            for c in range(3):
                turned[e + c, x] = h_out[e + c, x] - cut * curl[c]
    leaving = []
    for evolution in range(2):
        e, at = 3 * evolution, 2 * evolution * NY
        for x in range(NX):
            if x > 0:
                behind = [turned[e + c, x - 1][:NY] for c in (1, 2)]
            else:
                factor = edge_cut[:NY]
                behind = [
                    outer_local[pl.ds(at, NY), :] + factor * e_out[e + 2, 0][:NY],
                    outer_local[pl.ds(at + NY, NY), :] - factor * e_out[e + 1, 0][:NY],
                ]
            old = [e_out[e + c, x][:NY] for c in range(3)]
            new = last_e(old, rate[x], [turned[e + c, x] for c in range(3)], behind)
            if evolution:
                forward_old = [e_out[c, x][:NY] for c in range(3)]
                forward_new = [final_v[c, x] for c in range(3)]
                overlap[pl.ds(x * NY, NY), :] = product([forward_old, old], [forward_new, new])
            else:
                for c in range(3):
                    final_v[c, x] = new[c]
                if x % 4 == 3:
                    part = pl.ds(x - 3, 4)
                    leaving.append(
                        pltpu.make_async_copy(final_v.at[:, part], final.at[:, part], sems.at[10 + x // 4])
                    )
                    leaving[-1].start()

    def keep(x):
        for c in range(6):
            state[c] = e_out[c, x]
            state[6 + c] = turned[c, x]
        for evolution in range(2):
            for c in (1, 2):
                state[11 + 2 * evolution + c] = turned[3 * evolution + c, NX - 2]
        state[16, :NY] = rate[x]
        state[16, NY:] = nothing[NY:]

    pl.when(even)(lambda: keep(NX - 1))
    pl.when(jnp.logical_not(even))(lambda: keep(0))
    for copy in leaving:
        copy.wait()


def last_e(electric, scale, magnetic, behind):
    last_x, last_z = before_y(magnetic[0])[:NY], before_y(magnetic[2])[:NY]
    hx, hy, hz = [v[:NY] for v in magnetic]
    curl = (
        (hz - last_z) - (hy - before_z(hy)),
        (hx - before_z(hx)) - (hz - behind[1]),
        (hy - behind[0]) - (hx - last_x),
    )
    return [electric[c] + scale * curl[c] for c in range(3)]


def product(old, new):
    blend = math.cos(ANGULAR)
    total = 0.0
    for c in range(3):
        total += old[0][c] * (old[1][c] + blend * new[1][c])
        total += new[0][c] * (new[1][c] + blend * old[1][c])
    return total


def first_step(ef, hf, ea, ha, perm, inner, outer, inner_y, outer_y, message):
    return pl.pallas_call(
        step_one,
        out_shape=(
            shape(3, NX, NY, LANES),
            shape(NX * NY, LANES),
            shape(NX * 8, LANES),
            shape(17, EY, LANES),
            shape(PLANES * NY + 8, LANES),
        ),
        in_specs=[hbm()] * 5 + [anywhere()] * 5,
        out_specs=(hbm(),) + (vmem(),) * 4,
        scratch_shapes=[
            pltpu.VMEM((6, NX, EY, LANES), F32),
            pltpu.VMEM((6, NX, EY, LANES), F32),
            pltpu.VMEM((NX, EY, LANES), F32),
            pltpu.VMEM(((NX + 1) * EY, LANES), F32),
            pltpu.VMEM((6, NX, EY, LANES), F32),
            pltpu.VMEM((6, NX, EY, LANES), F32),
            pltpu.VMEM((6, NX, EY, LANES), F32),
            pltpu.VMEM((NX, NY, LANES), F32),
            pltpu.VMEM((3, NX, NY, LANES), F32),
            pltpu.VMEM((PLANES * NY + 8, LANES), F32),
            pltpu.VMEM(inner.shape, F32),
            pltpu.VMEM(outer.shape, F32),
            pltpu.VMEM(inner_y.shape, F32),
            pltpu.VMEM(outer_y.shape, F32),
            pltpu.VMEM(message.shape, F32),
            pltpu.SemaphoreType.DMA((14,)),
        ],
        compiler_params=params(51),
        cost_estimate=cost(5),
        name="step_one",
    )(ef, hf, ea, ha, perm, inner, outer, inner_y, outer_y, message)


def step_two(final_in, overlap_in, sigma_in, state, inner, message, final, reply, plane, overlap, sem):
    even = lax.axis_index("gx") % 2 == 0
    low_y = lax.axis_index("gy") > 0
    y = iota((EY, LANES), 0)
    cut = jnp.where(((y < EY - 2) | low_y) & even, COURANT, 0.0)
    x = jnp.where(even, NX - 1, 0)
    overlap[...] = overlap_in[...]
    old, new = [], []
    for evolution in range(2):
        e, at = 3 * evolution, 2 * evolution * NY
        rows = [inner[at + c * NY : at + (c + 1) * NY] for c in range(2)]
        beside = inner[PLANES * NY + evolution : PLANES * NY + evolution + 1]
        tile = jnp.where(iota((8, LANES), 0) == 7, beside, 0.0)
        ahead = [jnp.concatenate([r, tile], axis=0) for r in rows]
        old.append([state[e + c][:NY] for c in range(3)])
        magnetic = [state[6 + e], state[7 + e] + cut * ahead[1], state[8 + e] - cut * ahead[0]]
        behind = [
            jnp.where(even, state[12 + 2 * evolution][:NY], rows[0] + COURANT * old[-1][2]),
            jnp.where(even, state[13 + 2 * evolution][:NY], rows[1] - COURANT * old[-1][1]),
        ]
        new.append(last_e(old[-1], state[16][:NY], magnetic, behind))
    for c in range(3):
        plane[c] = new[0][c]
    final_copy = pltpu.make_async_copy(plane, final.at[:, x], sem)
    final_copy.start()
    overlap[pl.ds(pl.multiple_of(x * NY, NY), NY), :] = product(old, new)
    tiles = message.shape[0] // ROWS
    across = iota((tiles, LANES), 1)
    meta = [message[pl.ds(4 + k, tiles, stride=ROWS), :] for k in range(2)]
    block = NX * 8
    compact = jnp.zeros((block, LANES), F32)
    lane = iota((block, LANES), 1)
    for quarter in range(4):
        part = pltpu.roll(
            overlap[pl.ds(quarter, block, stride=4), :], (quarter * LAYERS - LOWER) % LANES, 1
        )
        compact = jnp.where(lane // LAYERS == quarter, part, compact)
    sigma = sigma_in[...]
    gradient = CONTRAST * sigma * (1.0 - sigma) * compact
    picks, shifts = [], []
    for k in range(2):
        starts = start_col(meta, k, 0)
        shifts.append(starts & (LANES - 1))
        for step in range(3):
            picks.append(jnp.where(iota((tiles, block), 1) == (starts >> 7) + step, 1.0, 0.0))
    found = select_rows(jnp.concatenate(picks, axis=0), gradient)
    for k in range(2):
        head, back, tail = [found[(3 * k + i) * tiles : (3 * k + i + 1) * tiles] for i in range(3)]
        reply[pl.ds(2 * k, tiles, stride=4), :] = jnp.where(across >= shifts[k], head, tail)
        reply[pl.ds(2 * k + 1, tiles, stride=4), :] = back
    final_copy.wait()


def second_step(final, overlap, sigma, state, inner, message):
    tiles = message.shape[0] // ROWS
    return pl.pallas_call(
        step_two,
        out_shape=(shape(3, NX, NY, LANES), shape(tiles * 4, LANES)),
        in_specs=[hbm()] + [vmem()] * 5,
        out_specs=(hbm(), vmem()),
        input_output_aliases={0: 0},
        scratch_shapes=[
            pltpu.VMEM((3, NY, LANES), F32),
            pltpu.VMEM((NX * NY, LANES), F32),
            pltpu.SemaphoreType.DMA,
        ],
        compiler_params=params(30),
        cost_estimate=cost(1),
        name="step_two",
    )(final, overlap, sigma, state, inner, message)


def unpack_tiles(reply, match, out):
    tiles = out.shape[0]
    shift = match[:, 2 * tiles : 2 * tiles + 1].astype(jnp.int32)
    count = match[:, 2 * tiles + 1 : 2 * tiles + 2].astype(jnp.int32)
    rows = [
        jnp.concatenate(
            [reply[pl.ds(2 * k + half, tiles, stride=4), :] for half in range(2)], axis=1
        )
        for k in range(2)
    ]
    cells = select_rows(match[:, : 2 * tiles], jnp.concatenate(rows, axis=0))
    width = out.shape[1]
    for bit in range(7):
        cells = jnp.where((shift >> bit) & 1 == 1, pltpu.roll(cells, width - (1 << bit), 1), cells)
    out[...] = jnp.where(iota(out.shape, 1) < count, cells, 0.0)


def unpack(reply, match):
    tiles = match.shape[0]
    return pl.pallas_call(
        unpack_tiles,
        out_shape=shape(tiles, 2 * LANES),
        in_specs=[vmem()] * 2,
        out_specs=vmem(),
        compiler_params=params(16),
        cost_estimate=cost(2),
        name="unpack_tiles",
    )(reply, match)


def swapped(block, axis, first):
    pairs = [(i, i + 1) for i in range(first, lax.axis_size(axis) - 1, 2)]
    return lax.ppermute(block, axis, pairs + [(j, i) for i, j in pairs])


def exchange(block, depth):
    out = lax.all_to_all(
        block.reshape(-1, depth, LANES), ("gx", "gy"), split_axis=0, concat_axis=0, tiled=True
    )
    return out.reshape(block.shape)


def faces_x(ef, hf, ea, ha, perm, inner_y, outer_y, inner_out, outer_out, first_x, last_x, edge_perm, tiles, sems):
    pairs = []
    for i, src in enumerate((ef, ea, hf, ha)):
        pairs.append((src.at[:, pl.ds(NX - 2, 2)], last_x.at[pl.ds(3 * i, 3)]))
        pairs.append((src.at[:, pl.ds(0, 2)], first_x.at[pl.ds(3 * i, 3)]))
    pairs.append((perm.at[NX - 1], edge_perm.at[0]))
    pairs.append((perm.at[0], edge_perm.at[1]))
    copies = [pltpu.make_async_copy(a, b, sems.at[i]) for i, (a, b) in enumerate(pairs)]
    for copy in copies:
        copy.start()
    beside = from_pairs("gy", inner_y, outer_y)
    for from_prev in (True, False):
        at = 0
        for evolution in range(2):
            for field, comp, begin, count in plan_y(from_prev):
                for k in range(count):
                    row = 8 + begin + k if from_prev else begin + k
                    for i, x in enumerate((NX - 2, NX - 1, 0, 1)):
                        tiles[field * 6 + evolution * 3 + comp, i, row : row + 1, :] = beside(
                            from_prev, at * NX + x, 1
                        )
                    at += 1
    for copy in copies:
        copy.wait()

    def plane(c, i):
        block = last_x[c, i] if i < 2 else first_x[c, i - 2]
        return jnp.concatenate([block, tiles[c, i]], axis=0)

    def send(out, planes, at, values):
        out[at * NY : (at + 1) * NY] = values[:NY]
        for k, row in enumerate(BESIDE):
            out[planes * NY + 3 * at + k : planes * NY + 3 * at + k + 1] = values[row : row + 1]

    def send_perm(out, planes, i, x):
        at = planes - 1
        out[at * NY : (at + 1) * NY] = edge_perm[i]
        for k, (from_prev, count) in enumerate(((True, UP_ROWS), (False, DOWN_ROWS))):
            begin = planes * NY + 3 * at + k
            out[begin : begin + 1] = beside(from_prev, (count - 1) * NX + x, 1)
        out[planes * TALL - 1 :] = jnp.zeros((outer_out.shape[0] - planes * TALL + 1, LANES), F32)

    inside_y = lax.axis_index("gy") > 0
    rate = jnp.where((iota((EY, LANES), 0) < EY - 2) | inside_y, COURANT, 0.0)
    nothing = jnp.zeros((EY, LANES), F32)

    def even_device():
        for evolution in range(2):
            e, h = 3 * evolution, 6 + 3 * evolution
            curl = curl_e([plane(e + c, 1) for c in range(3)], [nothing, nothing])
            for c in (1, 2):
                send(inner_out, PLANES, 2 * evolution + c - 1, plane(h + c, 1) - rate * curl[c])
            first, second = [[plane(e + c, i) for c in range(3)] for i in (2, 3)]
            curl = curl_e(first, second[1:])
            planes = first[1:] + [plane(h + c, 2) - rate * curl[c] for c in range(3)]
            for i, values in enumerate(planes):
                send(outer_out, DOWN_X, 5 * evolution + i, values)
        send_perm(outer_out, DOWN_X, 1, 0)

    def odd_device():
        for evolution in range(2):
            e, h = 3 * evolution, 6 + 3 * evolution
            for c in (1, 2):
                send(inner_out, PLANES, 2 * evolution + c - 1, plane(e + c, 2))
            before_last, last = [[plane(e + c, i) for c in range(3)] for i in (0, 1)]
            curl = curl_e(before_last, last[1:])
            planes = [plane(h + c, 0) - rate * curl[c] for c in (1, 2)]
            curl = curl_e(last, [nothing, nothing])
            planes = last + [plane(h + c, 1) - rate * curl[c] for c in range(3)] + planes
            for i, values in enumerate(planes):
                send(outer_out, UP_X, 8 * evolution + i, values)
        send_perm(outer_out, UP_X, 0, NX - 1)

    even = lax.axis_index("gx") % 2 == 0
    pl.when(even)(even_device)
    pl.when(jnp.logical_not(even))(odd_device)


def send_x(ef, hf, ea, ha, perm, inner_y, outer_y):
    return pl.pallas_call(
        faces_x,
        out_shape=(shape(PLANES * TALL, LANES), shape(UP_X * TALL, LANES)),
        in_specs=[hbm()] * 5 + [vmem()] * 2,
        out_specs=(vmem(), vmem()),
        scratch_shapes=[
            pltpu.VMEM((12, 2, NY, LANES), F32),
            pltpu.VMEM((12, 2, NY, LANES), F32),
            pltpu.VMEM((2, NY, LANES), F32),
            pltpu.VMEM((12, 4, 8, LANES), F32),
            pltpu.SemaphoreType.DMA((10,)),
        ],
        compiler_params=params(52),
        cost_estimate=cost(20),
        name="faces_x",
    )(ef, hf, ea, ha, perm, inner_y, outer_y)


def shards(ef, hf, ea, ha, perm, pattern, owners, tile_count, tile_start):
    inner_y, outer_y, message, match = prepare(
        ef, hf, ea, ha, perm, pattern, owners, tile_count, tile_start
    )
    outer_y, inner_y = swapped(outer_y, "gy", 1), swapped(inner_y, "gy", 0)
    arrived = exchange(message, 1)
    inner, outer = send_x(ef, hf, ea, ha, perm, inner_y, outer_y)
    outer, inner = swapped(outer, "gx", 1), swapped(inner, "gx", 0)
    *state, inner = first_step(
        ef, hf, ea, ha, perm, inner, outer, inner_y, outer_y, arrived
    )
    final, reply = second_step(*state, swapped(inner, "gx", 0), arrived)
    return final, unpack(exchange(reply, 4), match)


def solution(mesh):
    grid = P(None, "gx", "gy", None)
    tiles = ("gx", "gy")
    return jax.shard_map(
        shards,
        mesh=mesh,
        in_specs=(grid,) * 4 + (P("gx", "gy", None), P(tiles, None), P(tiles, None), P(tiles), P(tiles)),
        out_specs=(grid, P(tiles, None)),
        check_vma=False,
    )
```
